128 devices in a mesh: row: 8 (over z, y_lo), chan: 16 (over x, y_hi, core).
Axes of the slice: x: 4, y: 4 (y_hi: 2, y_lo: 2; y = y_hi * 2 + y_lo), z: 4, core: 2. Of those that a mesh axis runs over, the one named last changes fastest.
Arguments:
- pair: bfloat16 [128, 512, 512], P('chan', 'row'), may hold values from -6 to 6
- grad_out: bfloat16 [128, 512, 512], P('chan', 'row'), may hold values from -6 to 6
- residue_chain: int32 [512], replicated, may hold values from 0 to 4, as said below
- gain_in: float32 [2, 128], replicated, may hold values from 0.25 to 1.75
- w_in: bfloat16 [2, 128, 640], replicated, may hold values from -0.5 to 0.5
- gain_mid: float32 [2, 128], replicated, may hold values from 0.25 to 1.75
- w_out: bfloat16 [2, 128, 128], replicated, may hold values from -0.5 to 0.5
Outputs:
- pair_out: bfloat16 [128, 512, 512], P('chan', 'row')
- grad_pair: bfloat16 [128, 512, 512], P('chan', 'row')
- grad_gain_in: float32 [2, 128], replicated
- grad_w_in: float32 [2, 128, 640], replicated
- grad_gain_mid: float32 [2, 128], replicated
- grad_w_out: float32 [2, 128, 128], replicated
The draws below stay inside these ranges and needn't reach their ends.
Inputs may be any that keep to these rules, and one draw needn't show every extreme that they name: `residue_chain`: padding (0) fills a run of 1 to 64 residues at the end of the crop; every other residue is valid.
All inputs are finite; a program needn't handle non-finite values.
Results may differ from the reference program's by a relative error of at most 0.023.
Values may be sent and summed in bfloat16 or wider, within the bound.
A program may use at most 128 MiB of HBM per device.

```python
import jax
import jax.numpy as jnp
from jax import lax

C = 128
H = 128
N = 512


def draw_residue_chain(key, part):
    key = jax.random.fold_in(key, 7)
    key_pad, key_cut = jax.random.split(key)
    padding = jax.random.randint(key_pad, (), 1, N // 8 + 1)
    used_rows = N - padding
    jitter = jax.random.randint(key_cut, (3,), -(N // 16), N // 16 + 1)
    cuts = jnp.arange(1, 4, dtype=jnp.int32) * used_rows // 4 + jitter
    position = jnp.arange(N, dtype=jnp.int32)
    chains = 1 + jnp.sum((position[:, None] >= cuts[None, :]).astype(jnp.int32), axis=1)
    return jnp.where(position < used_rows, chains, 0).astype(jnp.int32)


def shard_levels(key, shape, shards, least, largest):
    level = 1.0
    for axis_at, parts in shards:
        draws = jax.random.uniform(jax.random.fold_in(jax.random.fold_in(key, 6), axis_at), (parts,), jnp.float32, least / len(shards), largest / len(shards))
        level = level * jnp.repeat(jnp.exp(draws), shape[axis_at] // parts).reshape((-1,) + (1,) * (len(shape) - 1 - axis_at))
    return level


def normal_values(stream_key, extent, scale, reach, cuts=(), held_as=jnp.bfloat16):
    drawn = scale * jax.random.normal(stream_key, extent, jnp.float32)
    if cuts:
        drawn = drawn * shard_levels(stream_key, extent, cuts, -0.22, 0.18)
    return jnp.clip(drawn, -reach, reach).astype(held_as)


def setup_inputs(seed: int = 0) -> dict:
    keys = jax.random.split(jax.random.key(seed), 8)
    return {
        "pair": normal_values(keys[0], (C, N, N), 1.0, 6.0, ((0, 16), (1, 8))),
        "grad_out": normal_values(keys[1], (C, N, N), 1.0, 6.0, ((0, 16), (1, 8))),
        "residue_chain": draw_residue_chain(jax.random.fold_in(keys[7], 71), 0),
        "gain_in": jnp.clip(1.0 + 0.15 * jax.random.normal(keys[3], (2, C), jnp.float32), 0.25, 1.75),
        "w_in": normal_values(keys[4], (2, C, 4 * H + C), C ** -0.5, 0.5),
        "gain_mid": jnp.clip(1.0 + 0.15 * jax.random.normal(keys[5], (2, H), jnp.float32), 0.25, 1.75),
        "w_out": normal_values(keys[6], (2, H, C), H ** -0.5, 0.5),
    }


epsilon = 1e-05
highest = lax.Precision.HIGHEST

def normalize(values, gain_vec):
    center = values - lax.optimization_barrier(jnp.mean(values, axis=0, keepdims=True))
    spread = lax.optimization_barrier(jnp.mean(center * center, axis=0, keepdims=True))
    return center * lax.rsqrt(spread + epsilon) * gain_vec[:, None, None]

def prepare(pair_f32, gain_vec, weight, mask_f):
    hidden_w = (weight.shape[1] - pair_f32.shape[0]) // 4
    normed = normalize(pair_f32, gain_vec)
    project = jnp.einsum('cd,cij->dij', weight, normed, precision=highest)
    left_proj = (mask_f * jax.nn.sigmoid(project[hidden_w:2 * hidden_w]) * project[:hidden_w]).astype(jnp.bfloat16)
    right_proj = (mask_f * jax.nn.sigmoid(project[3 * hidden_w:4 * hidden_w]) * project[2 * hidden_w:3 * hidden_w]).astype(jnp.bfloat16)
    gate_bf = jax.nn.sigmoid(project[4 * hidden_w:]).astype(jnp.bfloat16)
    return (left_proj, right_proj, gate_bf)

def finish(pair_f32, mixture, gate_bf, gain_vec, weight):
    normed = normalize(mixture.astype(jnp.float32), gain_vec)
    update = jnp.einsum('hc,hij->cij', weight, normed, precision=highest)
    return (pair_f32 + gate_bf.astype(jnp.float32) * update).astype(jnp.bfloat16)

def triangle(left_proj, right_proj, outgoing):
    left_f = left_proj.astype(jnp.float32)
    right_f = right_proj.astype(jnp.float32)
    if outgoing:
        product = jnp.einsum('hik,hjk->hij', left_f, right_f, precision=highest)
    else:
        product = jnp.einsum('hki,hkj->hij', left_f, right_f, precision=highest)
    return product.astype(jnp.bfloat16)

def forward(pair, gains_in, weights_in, gains_mid, weights_out, mask_f):
    field_now = pair
    for number, outgoing in ((0, True), (1, False)):
        pair_f32 = field_now.astype(jnp.float32)
        left_proj, right_proj, gate_bf = prepare(pair_f32, gains_in[number], weights_in[number], mask_f)
        mixture = triangle(left_proj, right_proj, outgoing)
        field_now = finish(pair_f32, mixture, gate_bf, gains_mid[number], weights_out[number])
    return field_now

def reference(pair, grad_out, residue_chain, gain_in, w_in, gain_mid, w_out):
    validity = (residue_chain > 0).astype(jnp.float32)
    mask_f = validity[:, None] * validity[None, :]

    def network(pair_in, gains_in, weights_in, gains_mid, weights_out):
        return forward(pair_in, gains_in, weights_in, gains_mid, weights_out, mask_f)
    pair_out, pullback = jax.vjp(network, pair, gain_in, w_in.astype(jnp.float32), gain_mid, w_out.astype(jnp.float32))
    grad_pair, grad_gi, grad_wi, grad_gm, grad_wo = pullback(grad_out)
    return (pair_out, grad_pair, grad_gi / N, grad_wi / N, grad_gm / N, grad_wo / N)
```

```python
from functools import partial

import jax
import jax.numpy as jnp
from jax import lax
from jax.sharding import PartitionSpec as P

epsilon = 1e-05


def normalize(values, gain_vec):
    center = values - jnp.mean(values, axis=0, keepdims=True)
    spread = jnp.mean(center * center, axis=0, keepdims=True)
    return center * lax.rsqrt(spread + epsilon) * gain_vec[:, None, None]


def prepare(pair_f32, gain_vec, weight, mask_f):
    hidden_w = (weight.shape[1] - pair_f32.shape[0]) // 4
    normed = normalize(pair_f32, gain_vec)
    project = jnp.einsum("cd,cij->dij", weight, normed)
    left_proj = (
        mask_f * jax.nn.sigmoid(project[hidden_w : 2 * hidden_w]) * project[:hidden_w]
    ).astype(jnp.bfloat16)
    right_proj = (
        mask_f
        * jax.nn.sigmoid(project[3 * hidden_w : 4 * hidden_w])
        * project[2 * hidden_w : 3 * hidden_w]
    ).astype(jnp.bfloat16)
    gate_bf = jax.nn.sigmoid(project[4 * hidden_w :]).astype(jnp.bfloat16)
    return (left_proj, right_proj, gate_bf)


def finish(pair_f32, mixture, gate_bf, gain_vec, weight):
    normed = normalize(mixture.astype(jnp.float32), gain_vec)
    update = jnp.einsum("hc,hij->cij", weight, normed)
    return (pair_f32 + gate_bf.astype(jnp.float32) * update).astype(jnp.bfloat16)


AXES = ("row", "chan")
ROWS = 16
COLS = 128


def to_cells(field):
    channels, rows, cols = field.shape
    tiles = field.reshape(channels, rows // ROWS, ROWS, cols // COLS, COLS).transpose(1, 3, 0, 2, 4)
    tiles = tiles.reshape(-1, ROWS, COLS)
    return lax.all_to_all(tiles, "chan", split_axis=0, concat_axis=0, tiled=True)


def from_cells(cells, rows, cols):
    tiles = lax.all_to_all(cells, "chan", split_axis=0, concat_axis=0, tiled=True)
    tiles = tiles.reshape(rows // ROWS, cols // COLS, -1, ROWS, COLS).transpose(2, 0, 3, 1, 4)
    return tiles.reshape(-1, rows, cols)


def to_hidden(cells, size):
    tiles = lax.all_to_all(cells, AXES, split_axis=0, concat_axis=0, tiled=True)
    tiles = tiles.reshape(size // ROWS, size // COLS, ROWS, COLS).transpose(0, 2, 1, 3)
    return tiles.reshape(size, size)


def to_tiles(matrix):
    size = matrix.shape[0]
    tiles = matrix.astype(jnp.bfloat16).reshape(size // ROWS, ROWS, size // COLS, COLS)
    tiles = tiles.transpose(0, 2, 1, 3).reshape(-1, ROWS, COLS)
    return lax.all_to_all(tiles, AXES, split_axis=0, concat_axis=0, tiled=True)


def mul(spec, a, b):
    return jnp.einsum(spec, a, b, preferred_element_type=jnp.float32)


def sum_all(values):
    flat = jnp.concatenate([v.reshape(-1) for v in values])
    parts = lax.all_to_all(flat.reshape(128, -1), AXES, split_axis=0, concat_axis=0, tiled=True)
    total = lax.all_gather(jnp.sum(parts, axis=0), AXES, axis=0, tiled=True)
    out, at = [], 0
    for v in values:
        out.append(total[at : at + v.size].reshape(v.shape))
        at += v.size
    return out


def local(pair, grad_out, residue_chain, gain_in, w_in, gain_mid, w_out):
    size = pair.shape[2]
    group = lax.axis_index("chan")
    first_row = lax.axis_index("row") * pair.shape[1] + (group // 4) * ROWS
    first_col = (group % 4) * COLS
    validity = (residue_chain > 0).astype(jnp.float32)
    mask_f = (
        lax.dynamic_slice_in_dim(validity, first_row, ROWS)[:, None]
        * lax.dynamic_slice_in_dim(validity, first_col, COLS)[None, :]
    )
    weights_in = w_in.astype(jnp.float32)
    weights_out = w_out.astype(jnp.float32)
    prepare_masked = partial(prepare, mask_f=mask_f)
    pair_zero = to_cells(pair).astype(jnp.float32)
    cotangent = to_cells(grad_out)
    left_zero, right_zero, gate_zero = prepare_masked(pair_zero, gain_in[0], weights_in[0])
    left_a, right_a = to_hidden(left_zero, size), to_hidden(right_zero, size)
    mix_zero = to_tiles(mul("ik,jk->ij", left_a, right_a))
    field_one = finish(pair_zero, mix_zero, gate_zero, gain_mid[0], weights_out[0])
    pair_one = field_one.astype(jnp.float32)
    left_one, right_one, gate_one = prepare_masked(pair_one, gain_in[1], weights_in[1])
    left_b, right_b = to_hidden(left_one, size), to_hidden(right_one, size)
    mix_one = to_tiles(mul("ki,kj->ij", left_b, right_b))
    field_two = finish(pair_one, mix_one, gate_one, gain_mid[1], weights_out[1])
    _, pull_finish_one = jax.vjp(
        finish, pair_one, mix_one, gate_one, gain_mid[1], weights_out[1]
    )
    dfield_fin1, dmix_one, dgate_one, dgm_one, dwo_one = pull_finish_one(cotangent)
    dmix_b = to_hidden(dmix_one, size)
    dleft_one = to_tiles(mul("kj,ij->ki", right_b, dmix_b))
    dright_one = to_tiles(mul("ki,ij->kj", left_b, dmix_b))
    _, pull_prepare_one = jax.vjp(prepare_masked, pair_one, gain_in[1], weights_in[1])
    dfield_pre1, dgi_one, dwi_one = pull_prepare_one((dleft_one, dright_one, dgate_one))
    grad_field_one = (dfield_fin1 + dfield_pre1).astype(jnp.bfloat16)
    _, pull_finish_zero = jax.vjp(
        finish, pair_zero, mix_zero, gate_zero, gain_mid[0], weights_out[0]
    )
    dfield_fin0, dmix_zero, dgate_zero, dgm_zero, dwo_zero = pull_finish_zero(grad_field_one)
    dmix_a = to_hidden(dmix_zero, size)
    dleft_zero = to_tiles(mul("ij,jk->ik", dmix_a, right_a))
    dright_zero = to_tiles(mul("ij,ik->jk", dmix_a, left_a))
    _, pull_prepare_zero = jax.vjp(prepare_masked, pair_zero, gain_in[0], weights_in[0])
    dfield_pre0, dgi_zero, dwi_zero = pull_prepare_zero((dleft_zero, dright_zero, dgate_zero))
    grad_field_zero = (dfield_fin0 + dfield_pre0).astype(jnp.bfloat16)
    pair_out = from_cells(field_two, pair.shape[1], size)
    grad_pair = from_cells(grad_field_zero, pair.shape[1], size)
    summed = sum_all(
        (
            jnp.stack([dgi_zero, dgi_one]),
            jnp.stack([dwi_zero, dwi_one]),
            jnp.stack([dgm_zero, dgm_one]),
            jnp.stack([dwo_zero, dwo_one]),
        )
    )
    factor = 1.0 / size
    return (pair_out, grad_pair) + tuple(v * factor for v in summed)


def solution(mesh):
    return jax.shard_map(
        local,
        mesh=mesh,
        in_specs=(P("chan", "row", None), P("chan", "row", None), P(), P(), P(), P(), P()),
        out_specs=(P("chan", "row", None), P("chan", "row", None), P(), P(), P(), P()),
        check_vma=False,
    )
```

```python
from functools import partial

import jax
import jax.numpy as jnp
from jax import lax
from jax.experimental import pallas as pl
from jax.experimental.pallas import tpu as pltpu
from jax.sharding import PartitionSpec as P

epsilon = 1e-05


def normalize(values, gain_vec):
    center = values - jnp.mean(values, axis=0, keepdims=True)
    spread = jnp.mean(center * center, axis=0, keepdims=True)
    return center * lax.rsqrt(spread + epsilon) * gain_vec[:, None, None]


def prepare(pair_f32, gain_vec, weight, mask_f):
    hidden_w = (weight.shape[1] - pair_f32.shape[0]) // 4
    normed = normalize(pair_f32, gain_vec)
    project = jnp.einsum("cd,cij->dij", weight, normed)
    left_proj = (
        mask_f * jax.nn.sigmoid(project[hidden_w : 2 * hidden_w]) * project[:hidden_w]
    ).astype(jnp.bfloat16)
    right_proj = (
        mask_f
        * jax.nn.sigmoid(project[3 * hidden_w : 4 * hidden_w])
        * project[2 * hidden_w : 3 * hidden_w]
    ).astype(jnp.bfloat16)
    gate_bf = jax.nn.sigmoid(project[4 * hidden_w :]).astype(jnp.bfloat16)
    return (left_proj, right_proj, gate_bf)


def finish(pair_f32, mixture, gate_bf, gain_vec, weight):
    normed = normalize(mixture.astype(jnp.float32), gain_vec)
    update = jnp.einsum("hc,hij->cij", weight, normed)
    return (pair_f32 + gate_bf.astype(jnp.float32) * update).astype(jnp.bfloat16)


ROWS = 16
COLS = 128


MESH = pl.DeviceIdType.MESH


def exchange_kernel(axes, gather, count, *refs):
    given, got = refs[:count], refs[count : 2 * count]
    send, recv, own = refs[2 * count :]
    row, chan = lax.axis_index("row"), lax.axis_index("chan")
    groups = lax.axis_size("chan")
    if axes == "chan":
        members, me = groups, chan
    else:
        members, me = groups * lax.axis_size("row"), row * groups + chan

    def place(to):
        return (row, to) if axes == "chan" else (to // groups, lax.rem(to, groups))

    barrier = pltpu.get_barrier_semaphore()

    def greet(step, carry):
        other = lax.rem(me + step, members)
        pl.semaphore_signal(barrier, inc=1, device_id=place(other), device_id_type=MESH)
        return carry

    lax.fori_loop(1, members, greet, 0)
    pl.semaphore_wait(barrier, members - 1)

    def dispatch(step, carry):
        other = lax.rem(me + step, members)
        for at, (src, dst) in enumerate(zip(given, got)):
            pltpu.make_async_remote_copy(
                src_ref=src.at[0] if gather else src.at[other],
                dst_ref=dst.at[me],
                send_sem=send.at[at],
                recv_sem=recv.at[at],
                device_id=place(other),
                device_id_type=MESH,
            ).start()
        return carry

    lax.fori_loop(1, members, dispatch, 0)
    for at, (src, dst) in enumerate(zip(given, got)):
        keep = pltpu.make_async_copy(src.at[0] if gather else src.at[me], dst.at[me], own)
        keep.start()
        keep.wait()
    for at, (src, dst) in enumerate(zip(given, got)):
        rest = dst.at[pl.ds(0, members - 1)]
        landed = pltpu.make_async_remote_copy(
            src_ref=rest,
            dst_ref=rest,
            send_sem=send.at[at],
            recv_sem=recv.at[at],
            device_id=(row, chan),
            device_id_type=MESH,
        )
        landed.wait_recv()
        landed.wait_send()


def exchange(ident, axes, *arrays, gather=False):
    members = 16 if axes == "chan" else 128
    count = len(arrays)
    space = pl.BlockSpec(memory_space=pl.ANY)
    return pl.pallas_call(
        partial(exchange_kernel, axes, gather, count),
        out_shape=[jax.ShapeDtypeStruct((members,) + a.shape[1:], a.dtype) for a in arrays],
        in_specs=[space] * count,
        out_specs=[space] * count,
        scratch_shapes=[
            pltpu.SemaphoreType.DMA((count,)),
            pltpu.SemaphoreType.DMA((count,)),
            pltpu.SemaphoreType.DMA,
        ],
        compiler_params=pltpu.CompilerParams(collective_id=ident, has_side_effects=True),
    )(*arrays)


def to_cells(field):
    channels, rows, cols = field.shape
    tiles = field.reshape(channels, rows // ROWS, ROWS, cols // COLS, COLS).transpose(1, 3, 0, 2, 4)
    tiles = tiles.reshape(-1, channels * ROWS, COLS)
    return exchange(0, "chan", tiles)[0].reshape(-1, ROWS, COLS)


def from_cells(cells, rows, cols):
    tiles = exchange(0, "chan", cells.reshape(16, -1, COLS))[0]
    tiles = tiles.reshape(rows // ROWS, cols // COLS, -1, ROWS, COLS).transpose(2, 0, 3, 1, 4)
    return tiles.reshape(-1, rows, cols)


def as_matrix(tiles, size):
    tiles = tiles.reshape(size // ROWS, size // COLS, ROWS, COLS).transpose(0, 2, 1, 3)
    return tiles.reshape(size, size)


def to_hidden(size, *cells):
    moved = exchange(len(cells), "all", *cells)
    return [as_matrix(t, size) for t in moved]


def as_tiles(matrix):
    size = matrix.shape[0]
    tiles = matrix.astype(jnp.bfloat16).reshape(size // ROWS, ROWS, size // COLS, COLS)
    return tiles.transpose(0, 2, 1, 3).reshape(-1, ROWS, COLS)


def to_tiles(*matrices):
    return exchange(len(matrices), "all", *[as_tiles(m) for m in matrices])


def mul(spec, a, b):
    return jnp.einsum(spec, a, b, preferred_element_type=jnp.float32)


def sum_all(values):
    flat = jnp.concatenate([v.reshape(-1) for v in values])
    room = 128 * ROWS * COLS
    flat = jnp.pad(flat, (0, room - flat.size)).reshape(128, ROWS, COLS)
    parts = exchange(3, "all", flat)[0]
    total = exchange(4, "all", jnp.sum(parts, axis=0, keepdims=True), gather=True)[0]
    total = total.reshape(-1)
    out, at = [], 0
    for v in values:
        out.append(total[at : at + v.size].reshape(v.shape))
        at += v.size
    return out


def local(pair, grad_out, residue_chain, gain_in, w_in, gain_mid, w_out):
    size = pair.shape[2]
    group = lax.axis_index("chan")
    first_row = lax.axis_index("row") * pair.shape[1] + (group // 4) * ROWS
    first_col = (group % 4) * COLS
    validity = (residue_chain > 0).astype(jnp.float32)
    mask_f = (
        lax.dynamic_slice_in_dim(validity, first_row, ROWS)[:, None]
        * lax.dynamic_slice_in_dim(validity, first_col, COLS)[None, :]
    )
    weights_in = w_in.astype(jnp.float32)
    weights_out = w_out.astype(jnp.float32)
    prepare_masked = partial(prepare, mask_f=mask_f)
    pair_zero = to_cells(pair).astype(jnp.float32)
    cotangent = to_cells(grad_out)
    left_zero, right_zero, gate_zero = prepare_masked(pair_zero, gain_in[0], weights_in[0])
    left_a, right_a = to_hidden(size, left_zero, right_zero)
    (mix_zero,) = to_tiles(mul("ik,jk->ij", left_a, right_a))
    field_one = finish(pair_zero, mix_zero, gate_zero, gain_mid[0], weights_out[0])
    pair_one = field_one.astype(jnp.float32)
    left_one, right_one, gate_one = prepare_masked(pair_one, gain_in[1], weights_in[1])
    left_b, right_b = to_hidden(size, left_one, right_one)
    (mix_one,) = to_tiles(mul("ki,kj->ij", left_b, right_b))
    field_two = finish(pair_one, mix_one, gate_one, gain_mid[1], weights_out[1])
    _, pull_finish_one = jax.vjp(
        finish, pair_one, mix_one, gate_one, gain_mid[1], weights_out[1]
    )
    dfield_fin1, dmix_one, dgate_one, dgm_one, dwo_one = pull_finish_one(cotangent)
    (dmix_b,) = to_hidden(size, dmix_one)
    dleft_one, dright_one = to_tiles(
        mul("kj,ij->ki", right_b, dmix_b), mul("ki,ij->kj", left_b, dmix_b)
    )
    _, pull_prepare_one = jax.vjp(prepare_masked, pair_one, gain_in[1], weights_in[1])
    dfield_pre1, dgi_one, dwi_one = pull_prepare_one((dleft_one, dright_one, dgate_one))
    grad_field_one = (dfield_fin1 + dfield_pre1).astype(jnp.bfloat16)
    _, pull_finish_zero = jax.vjp(
        finish, pair_zero, mix_zero, gate_zero, gain_mid[0], weights_out[0]
    )
    dfield_fin0, dmix_zero, dgate_zero, dgm_zero, dwo_zero = pull_finish_zero(grad_field_one)
    (dmix_a,) = to_hidden(size, dmix_zero)
    dleft_zero, dright_zero = to_tiles(
        mul("ij,jk->ik", dmix_a, right_a), mul("ij,ik->jk", dmix_a, left_a)
    )
    _, pull_prepare_zero = jax.vjp(prepare_masked, pair_zero, gain_in[0], weights_in[0])
    dfield_pre0, dgi_zero, dwi_zero = pull_prepare_zero((dleft_zero, dright_zero, dgate_zero))
    grad_field_zero = (dfield_fin0 + dfield_pre0).astype(jnp.bfloat16)
    pair_out = from_cells(field_two, pair.shape[1], size)
    grad_pair = from_cells(grad_field_zero, pair.shape[1], size)
    summed = sum_all(
        (
            jnp.stack([dgi_zero, dgi_one]),
            jnp.stack([dwi_zero, dwi_one]),
            jnp.stack([dgm_zero, dgm_one]),
            jnp.stack([dwo_zero, dwo_one]),
        )
    )
    factor = 1.0 / size
    return (pair_out, grad_pair) + tuple(v * factor for v in summed)


def solution(mesh):
    return jax.shard_map(
        local,
        mesh=mesh,
        in_specs=(P("chan", "row", None), P("chan", "row", None), P(), P(), P(), P(), P()),
        out_specs=(P("chan", "row", None), P("chan", "row", None), P(), P(), P(), P()),
        check_vma=False,
    )
```

```python
from functools import partial

import jax
import jax.numpy as jnp
from jax import lax
from jax.experimental import pallas as pl
from jax.experimental.pallas import tpu as pltpu
from jax.sharding import PartitionSpec as P

epsilon = 1e-05
MESH = pl.DeviceIdType.MESH
f32 = jnp.float32
bf16 = jnp.bfloat16

L0, R0, X0, L1, R1, X1, DX1, DL1, DR1, DX0, DL0, DR0 = range(12)
PAIR, GRAD, POUT, GOUT, SUM1, SUM0, ALL1, ALL0 = range(12, 20)
EXCHANGES = 20


def nn(a, b):
    return lax.dot_general(a, b, (((1,), (0,)), ((), ())), preferred_element_type=f32)


def nt(a, b):
    return lax.dot_general(a, b, (((1,), (1,)), ((), ())), preferred_element_type=f32)


def tn(a, b):
    return lax.dot_general(a, b, (((0,), (0,)), ((), ())), preferred_element_type=f32)


def sigmoid(x):
    return 0.5 * jnp.tanh(0.5 * x) + 0.5


def norm(z):
    center = z - jnp.mean(z, axis=0, keepdims=True)
    scale = lax.rsqrt(jnp.mean(center * center, axis=0, keepdims=True) + epsilon)
    return center * scale, scale


def norm_back(grad, normed, scale):
    mean_grad = jnp.mean(grad, axis=0, keepdims=True)
    mean_both = jnp.mean(grad * normed, axis=0, keepdims=True)
    return scale * (grad - mean_grad - normed * mean_both)


def kernel(
    dims,
    pair,
    grad,
    chain_s,
    chain_v,
    w_in,
    w_out,
    gain_in,
    gain_mid,
    pair_out,
    grad_pair,
    sum_in,
    sum_out,
    outbox,
    inbox,
    cells_out,
    cells_in,
    sums_out,
    sums_in,
    total,
    totals,
    wt,
    wn,
    wot,
    won,
    tile_a,
    tile_b,
    tile_g,
    field,
    zhat,
    zscale,
    xhat,
    xscale,
    value_l,
    sig_l,
    value_r,
    sig_r,
    gate,
    upd,
    du,
    dgate,
    dp,
    dz,
    send,
    recv,
    own,
):
    C, rows, J, groups, across, devices = dims
    per = 2
    chunks = rows // per
    wide = per * J
    row, chan = lax.axis_index("row"), lax.axis_index("chan")
    me = row * groups + chan
    tile_i, tile_j = chan // across, lax.rem(chan, across)

    def place(to):
        return (to // groups, lax.rem(to, groups))

    barrier = pltpu.get_barrier_semaphore()

    def greet(step, carry):
        other = lax.rem(me + step, devices)
        pl.semaphore_signal(barrier, inc=1, device_id=place(other), device_id_type=MESH)
        return carry

    lax.fori_loop(1, devices, greet, 0)
    pl.semaphore_wait(barrier, devices - 1)

    def scatter(at, src, dst):
        def step(k, carry):
            other = lax.rem(me + k, devices)
            pltpu.make_async_remote_copy(
                src_ref=src.at[other],
                dst_ref=dst.at[me],
                send_sem=send.at[at],
                recv_sem=recv.at[at],
                device_id=place(other),
                device_id_type=MESH,
            ).start()
            return carry

        lax.fori_loop(1, devices, step, 0)
        pltpu.make_async_copy(src.at[me], dst.at[me], own.at[at]).start()

    def spread(at, src, dst):
        def step(k, carry):
            other = lax.rem(me + k, devices)
            pltpu.make_async_remote_copy(
                src_ref=src,
                dst_ref=dst.at[me],
                send_sem=send.at[at],
                recv_sem=recv.at[at],
                device_id=place(other),
                device_id_type=MESH,
            ).start()
            return carry

        lax.fori_loop(1, devices, step, 0)
        pltpu.make_async_copy(src, dst.at[me], own.at[at]).start()

    def landed(at, like):
        rest = like.at[pl.ds(0, devices - 1)]
        return pltpu.make_async_remote_copy(
            src_ref=rest,
            dst_ref=rest,
            send_sem=send.at[at],
            recv_sem=recv.at[at],
            device_id=(row, chan),
            device_id_type=MESH,
        )

    def arrive(at, like):
        pltpu.make_async_copy(like.at[0], like.at[0], own.at[at]).wait()
        landed(at, like).wait_recv()

    own_c = C // groups

    def tile_of(ref, other):
        first = pl.multiple_of((other // across) * rows, rows)
        left = pl.multiple_of(lax.rem(other, across) * J, J)
        return ref.at[:, pl.ds(first, rows), pl.ds(left, J)]

    def channels(ref, other):
        return ref.at[pl.ds(pl.multiple_of(other * own_c, own_c), own_c)]

    def to_cells(at, src, dst):
        def step(k, carry):
            other = lax.rem(chan + k, groups)
            pltpu.make_async_remote_copy(
                src_ref=tile_of(src, other),
                dst_ref=channels(dst, chan),
                send_sem=send.at[at],
                recv_sem=recv.at[at],
                device_id=(row, other),
                device_id_type=MESH,
            ).start()
            return carry

        lax.fori_loop(1, groups, step, 0)
        pltpu.make_async_copy(tile_of(src, chan), channels(dst, chan), own.at[at]).start()

    def from_cells(at, src, dst):
        def step(k, carry):
            other = lax.rem(chan + k, groups)
            pltpu.make_async_remote_copy(
                src_ref=channels(src, other),
                dst_ref=tile_of(dst, chan),
                send_sem=send.at[at],
                recv_sem=recv.at[at],
                device_id=(row, other),
                device_id_type=MESH,
            ).start()
            return carry

        lax.fori_loop(1, groups, step, 0)
        pltpu.make_async_copy(channels(src, chan), tile_of(dst, chan), own.at[at]).start()

    def landed_chan(at, like):
        rest = like.at[pl.ds(0, C - own_c)]
        return pltpu.make_async_remote_copy(
            src_ref=rest,
            dst_ref=rest,
            send_sem=send.at[at],
            recv_sem=recv.at[at],
            device_id=(row, chan),
            device_id_type=MESH,
        )

    def arrive_chan(at, like):
        part = like.at[pl.ds(0, own_c)]
        pltpu.make_async_copy(part, part, own.at[at]).wait()
        landed_chan(at, like).wait_recv()

    block = C // 8

    def unpack(box, tile):
        @pl.loop(0, 8)
        def _(n):
            some = box[pl.ds(n * block, block)].astype(f32)
            first = pl.multiple_of(n * block * rows, block * rows)
            tile[pl.ds(first, block * rows), :] = some.reshape(block * rows, J)

    def pack(tile, box):
        @pl.loop(0, 8)
        def _(n):
            first = pl.multiple_of(n * block * rows, block * rows)
            some = tile[pl.ds(first, block * rows), :]
            box[pl.ds(n * block, block)] = some.reshape(block, rows, J).astype(bf16)

    def load(tile, n):
        return jnp.concatenate(
            [tile[pl.ds(n * per + s, C, stride=rows), :] for s in range(per)], axis=1
        )

    def store(tile, n, value):
        for s in range(per):
            tile[pl.ds(n * per + s, C, stride=rows), :] = value[:, s * J : (s + 1) * J]

    def lanes(n):
        return pl.ds(pl.multiple_of(n * wide, wide), wide)

    columns = (chain_v[pl.ds(tile_j, 1), :] > 0).astype(f32)
    first_row = row * (rows * groups // across) + tile_i * rows

    def mask(n):
        return jnp.concatenate(
            [
                columns * (chain_s[first_row + n * per + s] > 0).astype(f32)
                for s in range(per)
            ],
            axis=1,
        )

    def matrix(box):
        high = devices // across
        tiles = box[...].reshape(high, across, rows, J)
        return jnp.concatenate(
            [tiles[:, t].reshape(high * rows, J) for t in range(across)], axis=1
        )

    def to_tiles(value, box):
        high = devices // across
        value = value.astype(bf16)
        for i in range(high):
            for t in range(across):
                box[i * across + t] = value[i * rows : (i + 1) * rows, t * J : (t + 1) * J]

    to_cells(PAIR, pair, cells_in.at[0])
    to_cells(GRAD, grad, cells_in.at[1])
    for u in range(2):
        turned = jnp.transpose(w_in[u].astype(f32)) * gain_in[pl.ds(u, 1), :]
        wt[u] = turned.astype(bf16)
        wn[u] = jnp.transpose(turned).astype(bf16)
        turned = jnp.transpose(w_out[u].astype(f32)) * gain_mid[pl.ds(u, 1), :]
        wot[u] = turned.astype(bf16)
        won[u] = jnp.transpose(turned).astype(bf16)

    def side(u, n, at, value, sig, tile):
        p = nn(wt[u, 2 * at * C : 2 * (at + 1) * C, :], zhat[u, :, lanes(n)])
        v, s = p[:C], sigmoid(p[C:])
        value[u, :, lanes(n)] = v
        sig[u, :, lanes(n)] = s
        store(tile, n, mask(n) * s * v)

    def prepare(u, at_l, at_r):
        pack(tile_a, outbox.at[at_l])
        scatter(at_l, outbox.at[at_l], inbox.at[at_l])

        @pl.loop(0, chunks)
        def _(n):
            side(u, n, 1, value_r, sig_r, tile_b)

        pack(tile_b, outbox.at[at_r])
        scatter(at_r, outbox.at[at_r], inbox.at[at_r])

        @pl.loop(0, chunks)
        def _(n):
            p = nn(wt[u, 4 * C :, :], zhat[u, :, lanes(n)])
            gate[u, :, lanes(n)] = sigmoid(p).astype(bf16).astype(f32)

    arrive_chan(PAIR, cells_in.at[0])
    unpack(cells_in.at[0], tile_b)

    @pl.loop(0, chunks)
    def _(n):
        z = load(tile_b, n)
        field[0, :, lanes(n)] = z
        normed, scale = norm(z)
        zhat[0, :, lanes(n)] = normed.astype(bf16)
        zscale[0, :, lanes(n)] = scale
        side(0, n, 0, value_l, sig_l, tile_a)

    prepare(0, L0, R0)
    arrive_chan(GRAD, cells_in.at[1])
    unpack(cells_in.at[1], tile_g)

    arrive(L0, inbox.at[L0])
    arrive(R0, inbox.at[R0])
    to_tiles(nt(matrix(inbox.at[L0]), matrix(inbox.at[R0])), outbox.at[X0])
    scatter(X0, outbox.at[X0], inbox.at[X0])

    arrive(X0, inbox.at[X0])
    unpack(inbox.at[X0], tile_b)

    @pl.loop(0, chunks)
    def _(n):
        normed, scale = norm(load(tile_b, n))
        normed = normed.astype(bf16)
        xhat[0, :, lanes(n)] = normed
        xscale[0, :, lanes(n)] = scale
        update = nn(wot[0], normed)
        upd[:, lanes(n)] = update
        z = (field[0, :, lanes(n)] + gate[0, :, lanes(n)] * update).astype(bf16).astype(f32)
        field[1, :, lanes(n)] = z
        normed, scale = norm(z)
        zhat[1, :, lanes(n)] = normed.astype(bf16)
        zscale[1, :, lanes(n)] = scale
        side(1, n, 0, value_l, sig_l, tile_a)

    prepare(1, L1, R1)
    arrive(L1, inbox.at[L1])
    arrive(R1, inbox.at[R1])
    to_tiles(tn(matrix(inbox.at[L1]), matrix(inbox.at[R1])), outbox.at[X1])
    scatter(X1, outbox.at[X1], inbox.at[X1])

    arrive(X1, inbox.at[X1])
    unpack(inbox.at[X1], tile_b)

    def finish_back(u, n, cotangent, update):
        dgate[:, lanes(n)] = (cotangent * update).astype(bf16).astype(f32)
        back = (cotangent * gate[u, :, lanes(n)]).astype(bf16)
        du[u, :, lanes(n)] = back
        dx = norm_back(nn(won[u], back), xhat[u, :, lanes(n)].astype(f32), xscale[u, :, lanes(n)])
        store(tile_a, n, dx)

    @pl.loop(0, chunks)
    def _(n):
        normed, scale = norm(load(tile_b, n))
        normed = normed.astype(bf16)
        xhat[1, :, lanes(n)] = normed
        xscale[1, :, lanes(n)] = scale
        update = nn(wot[1], normed)
        cotangent = load(tile_g, n)
        store(tile_b, n, field[1, :, lanes(n)] + gate[1, :, lanes(n)] * update)
        finish_back(1, n, cotangent, update)

    pack(tile_a, outbox.at[DX1])
    scatter(DX1, outbox.at[DX1], inbox.at[DX1])
    pack(tile_b, cells_out.at[0])
    from_cells(POUT, cells_out.at[0], pair_out)

    arrive(DX1, inbox.at[DX1])
    to_tiles(nt(matrix(inbox.at[R1]), matrix(inbox.at[DX1])), outbox.at[DL1])
    scatter(DL1, outbox.at[DL1], inbox.at[DL1])
    to_tiles(nn(matrix(inbox.at[L1]), matrix(inbox.at[DX1])), outbox.at[DR1])
    scatter(DR1, outbox.at[DR1], inbox.at[DR1])

    def side_back(u, n, at, value, sig, tile):
        s = sig[u, :, lanes(n)]
        back = load(tile, n) * mask(n) * s
        dp[2 * at * C : (2 * at + 1) * C, lanes(n)] = back.astype(bf16)
        back = back * value[u, :, lanes(n)] * (1.0 - s)
        dp[(2 * at + 1) * C : 2 * (at + 1) * C, lanes(n)] = back.astype(bf16)

    def gate_back(u):
        @pl.loop(0, chunks)
        def _(n):
            s = gate[u, :, lanes(n)]
            dp[4 * C :, lanes(n)] = (dgate[:, lanes(n)] * s * (1.0 - s)).astype(bf16)

    def left_back(u, at):
        gate_back(u)
        arrive(at, inbox.at[at])
        unpack(inbox.at[at], tile_a)

        @pl.loop(0, chunks)
        def _(n):
            side_back(u, n, 0, value_l, sig_l, tile_a)

    def prepare_back(u, n):
        grad_z = nn(wn[u], dp[:, lanes(n)])
        return norm_back(grad_z, zhat[u, :, lanes(n)].astype(f32), zscale[u, :, lanes(n)])

    left_back(1, DL1)
    arrive(DR1, inbox.at[DR1])
    unpack(inbox.at[DR1], tile_b)

    @pl.loop(0, chunks)
    def _(n):
        side_back(1, n, 1, value_r, sig_r, tile_b)
        cotangent = (load(tile_g, n) + prepare_back(1, n)).astype(bf16).astype(f32)
        dz[:, lanes(n)] = cotangent
        finish_back(0, n, cotangent, upd[:, lanes(n)])

    pack(tile_a, outbox.at[DX0])
    scatter(DX0, outbox.at[DX0], inbox.at[DX0])

    def lay(box, at, value):
        for t in range(value.shape[1] // C):
            box[pl.ds(at + t, C, stride=8), :] = value[:, t * C : (t + 1) * C]

    def send_sums(at, which, tile):
        @pl.loop(0, 8)
        def _(n):
            some = tile[pl.ds(pl.multiple_of(n * block * 8, block * 8), block * 8), :]
            sums_out[which, pl.ds(n * block, block)] = some.reshape(block, 8, C)

        scatter(at, sums_out.at[which], sums_in.at[which])

    def add_sums(at_in, at_out, which):
        arrive(at_in, sums_in.at[which])
        total[which] = jnp.sum(sums_in[which], axis=0)
        spread(at_out, total.at[which], totals.at[which])

    lay(tile_b, 0, nt(zhat[1], dp[...]))
    lay(tile_b, 5, nt(xhat[1], du[1]))
    lay(tile_b, 6, nt(xhat[0], du[0]))
    lay(tile_b, 7, jnp.zeros((C, C), f32))
    send_sums(SUM1, 0, tile_b)

    arrive(DX0, inbox.at[DX0])
    to_tiles(nn(matrix(inbox.at[DX0]), matrix(inbox.at[R0])), outbox.at[DL0])
    scatter(DL0, outbox.at[DL0], inbox.at[DL0])
    to_tiles(tn(matrix(inbox.at[DX0]), matrix(inbox.at[L0])), outbox.at[DR0])
    scatter(DR0, outbox.at[DR0], inbox.at[DR0])
    add_sums(SUM1, ALL1, 0)

    left_back(0, DL0)
    arrive(DR0, inbox.at[DR0])
    unpack(inbox.at[DR0], tile_b)

    @pl.loop(0, chunks)
    def _(n):
        side_back(0, n, 1, value_r, sig_r, tile_b)

    lay(tile_b, 0, nt(zhat[0], dp[...]))
    for t in range(5, 8):
        lay(tile_b, t, jnp.zeros((C, C), f32))
    send_sums(SUM0, 1, tile_b)

    @pl.loop(0, chunks)
    def _(n):
        store(tile_a, n, dz[:, lanes(n)] + prepare_back(0, n))

    pack(tile_a, cells_out.at[1])
    from_cells(GOUT, cells_out.at[1], grad_pair)
    add_sums(SUM0, ALL0, 1)

    def take(which, t):
        @pl.loop(0, 8)
        def _(n):
            some = totals[which, pl.ds(n * block, block)].reshape(block * 8, C)
            tile_b[pl.ds(pl.multiple_of(n * block * 8, block * 8), block * 8), :] = some

    def fetch(t):
        return tile_b[pl.ds(t, C, stride=8), :]

    arrive(ALL1, totals.at[0])
    take(0, 0)
    for t in range(5):
        sum_in[1, :, t * C : (t + 1) * C] = fetch(t)
    sum_out[1] = fetch(5)
    sum_out[0] = fetch(6)
    arrive(ALL0, totals.at[1])
    take(1, 0)
    for t in range(5):
        sum_in[0, :, t * C : (t + 1) * C] = fetch(t)

    arrive_chan(POUT, cells_out.at[0])
    arrive_chan(GOUT, cells_out.at[1])
    for at in range(12):
        landed(at, outbox.at[at]).wait_send()
    for at in range(PAIR, SUM1):
        landed_chan(at, cells_out.at[0]).wait_send()
    for at in range(SUM1, EXCHANGES):
        landed(at, sums_out.at[0]).wait_send()


def local(groups, pair, grad_out, residue_chain, gain_in, w_in, gain_mid, w_out):
    C = w_in.shape[1]
    own_c, own_rows, size = pair.shape
    devices = C
    across = 4 if groups == 16 else 2
    J = size // across
    rows = own_rows * across // groups
    cells = rows * J
    dims = (C, rows, J, groups, across, devices)
    whole = pl.BlockSpec(memory_space=pltpu.VMEM)
    far = pl.BlockSpec(memory_space=pl.ANY)
    box = (C, rows, J)
    got = pl.pallas_call(
        partial(kernel, dims),
        out_shape=[
            jax.ShapeDtypeStruct(pair.shape, bf16),
            jax.ShapeDtypeStruct(pair.shape, bf16),
            jax.ShapeDtypeStruct(w_in.shape, f32),
            jax.ShapeDtypeStruct(w_out.shape, f32),
        ],
        in_specs=[far, far, pl.BlockSpec(memory_space=pltpu.SMEM)] + [whole] * 5,
        out_specs=[far, far, whole, whole],
        scratch_shapes=[
            pltpu.VMEM((12,) + box, bf16),
            pltpu.VMEM((12,) + box, bf16),
            pltpu.VMEM((2,) + box, bf16),
            pltpu.VMEM((2,) + box, bf16),
            pltpu.VMEM((2, C, 8, C), f32),
            pltpu.VMEM((2, C, 8, C), f32),
            pltpu.VMEM((2, 8, C), f32),
            pltpu.VMEM((2, C, 8, C), f32),
            pltpu.VMEM((2, 5 * C, C), bf16),
            pltpu.VMEM((2, C, 5 * C), bf16),
            pltpu.VMEM((2, C, C), bf16),
            pltpu.VMEM((2, C, C), bf16),
            pltpu.VMEM((C * rows, J), f32),
            pltpu.VMEM((C * rows, J), f32),
            pltpu.VMEM((C * rows, J), f32),
            pltpu.VMEM((2, C, cells), f32),
            pltpu.VMEM((2, C, cells), bf16),
            pltpu.VMEM((2, 1, cells), f32),
            pltpu.VMEM((2, C, cells), bf16),
            pltpu.VMEM((2, 1, cells), f32),
            pltpu.VMEM((2, C, cells), f32),
            pltpu.VMEM((2, C, cells), f32),
            pltpu.VMEM((2, C, cells), f32),
            pltpu.VMEM((2, C, cells), f32),
            pltpu.VMEM((2, C, cells), f32),
            pltpu.VMEM((C, cells), f32),
            pltpu.VMEM((2, C, cells), bf16),
            pltpu.VMEM((C, cells), f32),
            pltpu.VMEM((5 * C, cells), bf16),
            pltpu.VMEM((C, cells), f32),
            pltpu.SemaphoreType.DMA((EXCHANGES,)),
            pltpu.SemaphoreType.DMA((EXCHANGES,)),
            pltpu.SemaphoreType.DMA((EXCHANGES,)),
        ],
        compiler_params=pltpu.CompilerParams(
            collective_id=0, has_side_effects=True, vmem_limit_bytes=60 * 2**20
        ),
    )(
        pair,
        grad_out,
        residue_chain,
        residue_chain.reshape(across, J),
        w_in,
        w_out,
        gain_in,
        gain_mid,
    )
    pair_out, grad_pair, sum_in, sum_out = got
    factor = 1.0 / size
    return (
        pair_out,
        grad_pair,
        jnp.sum(sum_in * w_in.astype(f32), axis=2) * factor,
        sum_in * gain_in[:, :, None] * factor,
        jnp.sum(sum_out * w_out.astype(f32), axis=2) * factor,
        sum_out * gain_mid[:, :, None] * factor,
    )


def solution(mesh):
    return jax.shard_map(
        partial(local, mesh.shape["chan"]),
        mesh=mesh,
        in_specs=(P("chan", "row", None), P("chan", "row", None), P(), P(), P(), P(), P()),
        out_specs=(P("chan", "row", None), P("chan", "row", None), P(), P(), P(), P()),
        check_vma=False,
    )
```

```python
from functools import partial

import jax
import jax.numpy as jnp
from jax import lax
from jax.experimental import pallas as pl
from jax.experimental.pallas import tpu as pltpu
from jax.sharding import PartitionSpec as P

epsilon = 1e-05
MESH = pl.DeviceIdType.MESH
f32 = jnp.float32
bf16 = jnp.bfloat16

L0, R0, X0, L1, R1, X1, DX1, DL1, DR1, DX0, DL0, DR0 = range(12)
PAIR, GRAD, POUT, GOUT = range(12, 16)
CORES, SCATTER, GATHER, SHARE = range(16, 20)
EXCHANGES = 20
AT_IN = (7, 0)
AT_OUT = (6, 5)
SUM_ROWS = 16


def nn(a, b):
    return lax.dot_general(a, b, (((1,), (0,)), ((), ())), preferred_element_type=f32)


def nt(a, b):
    return lax.dot_general(a, b, (((1,), (1,)), ((), ())), preferred_element_type=f32)


def tn(a, b):
    return lax.dot_general(a, b, (((0,), (0,)), ((), ())), preferred_element_type=f32)


def sigmoid(x):
    return 0.5 * jnp.tanh(0.5 * x) + 0.5


def norm(z):
    center = z - jnp.mean(z, axis=0, keepdims=True)
    scale = lax.rsqrt(jnp.mean(center * center, axis=0, keepdims=True) + epsilon)
    return center * scale, scale


def norm_back(grad, normed, scale):
    mean_grad = jnp.mean(grad, axis=0, keepdims=True)
    mean_both = jnp.mean(grad * normed, axis=0, keepdims=True)
    return scale * (grad - mean_grad - normed * mean_both)


def kernel(
    dims,
    pair,
    grad,
    chain_s,
    chain_v,
    w_in,
    w_out,
    gain_in,
    gain_mid,
    pair_out,
    grad_pair,
    d_gain_in,
    d_w_in,
    d_gain_mid,
    d_w_out,
    outbox,
    inbox,
    cells_out,
    cells_in,
    sums,
    sums_core,
    sums_chip,
    sums_in,
    total,
    totals,
    tile_s,
    wt,
    wn,
    wot,
    won,
    tile_a,
    tile_b,
    tile_g,
    field,
    zhat,
    zscale,
    xhat,
    xscale,
    value_l,
    sig_l,
    value_r,
    sig_r,
    gate,
    upd,
    du,
    part,
    dp,
    dz,
    send,
    recv,
    own,
):
    C, rows, J, groups, across, devices = dims
    per = 8
    chunks = rows // per
    wide = per * J
    row, chan = lax.axis_index("row"), lax.axis_index("chan")
    me = row * groups + chan
    tile_i, tile_j = chan // across, lax.rem(chan, across)

    def place(to):
        return (to // groups, lax.rem(to, groups))

    barrier = pltpu.get_barrier_semaphore()

    def greet(step, carry):
        other = lax.rem(me + step, devices)
        pl.semaphore_signal(barrier, inc=1, device_id=place(other), device_id_type=MESH)
        return carry

    lax.fori_loop(1, devices, greet, 0)
    pl.semaphore_wait(barrier, devices - 1)

    def scatter(at, src, dst):
        def step(k, carry):
            other = lax.rem(me + k, devices)
            pltpu.make_async_remote_copy(
                src_ref=src.at[other],
                dst_ref=dst.at[me],
                send_sem=send.at[at],
                recv_sem=recv.at[at],
                device_id=place(other),
                device_id_type=MESH,
            ).start()
            return carry

        lax.fori_loop(1, devices, step, 0)
        pltpu.make_async_copy(src.at[me], dst.at[me], own.at[at]).start()

    chips, core = devices // 2, lax.rem(me, 2)
    chip = me // 2

    def over_chips(at, source, dst):
        def step(k, carry):
            other = lax.rem(chip + k, chips)
            pltpu.make_async_remote_copy(
                src_ref=source(other),
                dst_ref=dst,
                send_sem=send.at[at],
                recv_sem=recv.at[at],
                device_id=place(2 * other + core),
                device_id_type=MESH,
            ).start()
            return carry

        lax.fori_loop(1, chips, step, 0)

    def to_sibling(at, src, dst):
        return pltpu.make_async_remote_copy(
            src_ref=src,
            dst_ref=dst,
            send_sem=send.at[at],
            recv_sem=recv.at[at],
            device_id=place(2 * chip + 1 - core),
            device_id_type=MESH,
        )

    def landed_chips(at):
        rest = sums_in.at[pl.ds(0, chips - 1)]
        return to_sibling(at, rest, rest)

    def landed(at, like):
        rest = like.at[pl.ds(0, devices - 1)]
        return pltpu.make_async_remote_copy(
            src_ref=rest,
            dst_ref=rest,
            send_sem=send.at[at],
            recv_sem=recv.at[at],
            device_id=(row, chan),
            device_id_type=MESH,
        )

    def arrive(at, like):
        pltpu.make_async_copy(like.at[0], like.at[0], own.at[at]).wait()
        landed(at, like).wait_recv()

    own_c = C // groups
    every = (0, groups)
    quarters = [(q * groups // 4, (q + 1) * groups // 4) for q in range(4)]

    def tile_of(ref, other):
        first = pl.multiple_of((other // across) * rows, rows)
        left = pl.multiple_of(lax.rem(other, across) * J, J)
        return ref.at[:, pl.ds(first, rows), pl.ds(left, J)]

    def channels(ref, other):
        return ref.at[pl.ds(pl.multiple_of(other * own_c, own_c), own_c)]

    def to_cells(at, src, dst, piece):
        def step(k, carry):
            other = lax.rem(chan + k, groups)
            pltpu.make_async_remote_copy(
                src_ref=tile_of(src, other),
                dst_ref=channels(dst, chan),
                send_sem=send.at[at],
                recv_sem=recv.at[at],
                device_id=(row, other),
                device_id_type=MESH,
            ).start()
            return carry

        lax.fori_loop(max(1, piece[0]), piece[1], step, 0)
        if piece[0] == 0:
            pltpu.make_async_copy(tile_of(src, chan), channels(dst, chan), own.at[at]).start()

    def from_cells(at, src, dst, piece):
        def step(k, carry):
            other = lax.rem(chan + k, groups)
            pltpu.make_async_remote_copy(
                src_ref=channels(src, other),
                dst_ref=tile_of(dst, chan),
                send_sem=send.at[at],
                recv_sem=recv.at[at],
                device_id=(row, other),
                device_id_type=MESH,
            ).start()
            return carry

        lax.fori_loop(max(1, piece[0]), piece[1], step, 0)
        if piece[0] == 0:
            pltpu.make_async_copy(channels(src, chan), tile_of(dst, chan), own.at[at]).start()

    def landed_chan(at, like):
        rest = like.at[pl.ds(0, C - own_c)]
        return pltpu.make_async_remote_copy(
            src_ref=rest,
            dst_ref=rest,
            send_sem=send.at[at],
            recv_sem=recv.at[at],
            device_id=(row, chan),
            device_id_type=MESH,
        )

    def arrive_chan(at, like):
        part = like.at[pl.ds(0, own_c)]
        pltpu.make_async_copy(part, part, own.at[at]).wait()
        landed_chan(at, like).wait_recv()

    block = C // 8

    def unpack(box, tile):
        @pl.loop(0, 8)
        def _(n):
            some = box[pl.ds(n * block, block)].astype(f32)
            first = pl.multiple_of(n * block * rows, block * rows)
            tile[pl.ds(first, block * rows), :] = some.reshape(block * rows, J)

    def pack(tile, box):
        @pl.loop(0, 8)
        def _(n):
            first = pl.multiple_of(n * block * rows, block * rows)
            some = tile[pl.ds(first, block * rows), :]
            box[pl.ds(n * block, block)] = some.reshape(block, rows, J).astype(bf16)

    def load(tile, n):
        return jnp.concatenate(
            [tile[pl.ds(n * per + s, C, stride=rows), :] for s in range(per)], axis=1
        )

    def store(tile, n, value):
        for s in range(per):
            tile[pl.ds(n * per + s, C, stride=rows), :] = value[:, s * J : (s + 1) * J]

    def lanes(n):
        return pl.ds(pl.multiple_of(n * wide, wide), wide)

    columns = (chain_v[pl.ds(tile_j, 1), :] > 0).astype(f32)
    first_row = row * (rows * groups // across) + tile_i * rows

    def mask(n):
        return jnp.concatenate(
            [
                columns * (chain_s[first_row + n * per + s] > 0).astype(f32)
                for s in range(per)
            ],
            axis=1,
        )

    def matrix(box):
        high = devices // across
        tiles = box[...].reshape(high, across, rows, J)
        return jnp.concatenate(
            [tiles[:, t].reshape(high * rows, J) for t in range(across)], axis=1
        )

    def to_tiles(value, box):
        high = devices // across
        value = value.astype(bf16)
        for i in range(high):
            for t in range(across):
                box[i * across + t] = value[i * rows : (i + 1) * rows, t * J : (t + 1) * J]

    to_cells(PAIR, pair, cells_in.at[0], every)
    to_cells(GRAD, grad, cells_in.at[1], quarters[0])
    for u in range(2):
        turned = jnp.transpose(w_in[u].astype(f32)) * gain_in[pl.ds(u, 1), :]
        wt[u] = turned.astype(bf16)
        wn[u] = jnp.transpose(turned).astype(bf16)
        turned = jnp.transpose(w_out[u].astype(f32)) * gain_mid[pl.ds(u, 1), :]
        wot[u] = turned.astype(bf16)
        won[u] = jnp.transpose(turned).astype(bf16)

    def side(u, n, at, value, sig, tile):
        p = nn(wt[u, 2 * at * C : 2 * (at + 1) * C, :], zhat[u, :, lanes(n)])
        v, s = p[:C], sigmoid(p[C:])
        value[u, :, lanes(n)] = v
        sig[u, :, lanes(n)] = s
        store(tile, n, mask(n) * s * v)

    def prepare(u, at_l, at_r):
        pack(tile_a, outbox.at[at_l])
        scatter(at_l, outbox.at[at_l], inbox.at[at_l])

        @pl.loop(0, chunks)
        def _(n):
            side(u, n, 1, value_r, sig_r, tile_b)

        pack(tile_b, outbox.at[at_r])
        scatter(at_r, outbox.at[at_r], inbox.at[at_r])

        @pl.loop(0, chunks)
        def _(n):
            p = nn(wt[u, 4 * C :, :], zhat[u, :, lanes(n)])
            gate[u, :, lanes(n)] = sigmoid(p).astype(bf16).astype(f32)

    arrive_chan(PAIR, cells_in.at[0])
    unpack(cells_in.at[0], tile_b)

    @pl.loop(0, chunks)
    def _(n):
        z = load(tile_b, n)
        field[0, :, lanes(n)] = z
        normed, scale = norm(z)
        zhat[0, :, lanes(n)] = normed.astype(bf16)
        zscale[0, :, lanes(n)] = scale
        side(0, n, 0, value_l, sig_l, tile_a)

    prepare(0, L0, R0)
    to_cells(GRAD, grad, cells_in.at[1], quarters[1])
    arrive(L0, inbox.at[L0])
    arrive(R0, inbox.at[R0])
    to_tiles(nt(matrix(inbox.at[L0]), matrix(inbox.at[R0])), outbox.at[X0])
    scatter(X0, outbox.at[X0], inbox.at[X0])
    to_cells(GRAD, grad, cells_in.at[1], quarters[2])

    arrive(X0, inbox.at[X0])
    unpack(inbox.at[X0], tile_b)

    @pl.loop(0, chunks)
    def _(n):
        normed, scale = norm(load(tile_b, n))
        normed = normed.astype(bf16)
        xhat[0, :, lanes(n)] = normed
        xscale[:, lanes(n)] = scale
        update = nn(wot[0], normed)
        upd[:, lanes(n)] = update
        z = (field[0, :, lanes(n)] + gate[0, :, lanes(n)] * update).astype(bf16).astype(f32)
        field[1, :, lanes(n)] = z
        normed, scale = norm(z)
        zhat[1, :, lanes(n)] = normed.astype(bf16)
        zscale[1, :, lanes(n)] = scale
        side(1, n, 0, value_l, sig_l, tile_a)

    prepare(1, L1, R1)
    to_cells(GRAD, grad, cells_in.at[1], quarters[3])
    arrive(L1, inbox.at[L1])
    arrive(R1, inbox.at[R1])
    to_tiles(tn(matrix(inbox.at[L1]), matrix(inbox.at[R1])), outbox.at[X1])
    scatter(X1, outbox.at[X1], inbox.at[X1])
    arrive_chan(GRAD, cells_in.at[1])
    unpack(cells_in.at[1], tile_g)

    def finish_back(u, n, cotangent):
        back = (cotangent * gate[u, :, lanes(n)]).astype(bf16)
        du[u, :, lanes(n)] = back
        return nn(won[u], back)

    @pl.loop(0, chunks)
    def _(n):
        part[:, lanes(n)] = finish_back(1, n, load(tile_g, n))

    arrive(X1, inbox.at[X1])
    unpack(inbox.at[X1], tile_b)

    @pl.loop(0, chunks)
    def _(n):
        normed, scale = norm(load(tile_b, n))
        xhat[1, :, lanes(n)] = normed.astype(bf16)
        store(tile_a, n, norm_back(part[:, lanes(n)], normed, scale))

    pack(tile_a, outbox.at[DX1])
    scatter(DX1, outbox.at[DX1], inbox.at[DX1])

    def gate_back(u, n, cotangent, update):
        s = gate[u, :, lanes(n)]
        back = (cotangent * update).astype(bf16).astype(f32)
        dp[4 * C :, lanes(n)] = (back * s * (1.0 - s)).astype(bf16)

    @pl.loop(0, chunks)
    def _(n):
        update = nn(wot[1], xhat[1, :, lanes(n)])
        store(tile_b, n, field[1, :, lanes(n)] + gate[1, :, lanes(n)] * update)
        gate_back(1, n, load(tile_g, n), update)

    pack(tile_b, cells_out.at[0])
    from_cells(POUT, cells_out.at[0], pair_out, quarters[0])

    arrive(DX1, inbox.at[DX1])
    to_tiles(nt(matrix(inbox.at[R1]), matrix(inbox.at[DX1])), outbox.at[DL1])
    scatter(DL1, outbox.at[DL1], inbox.at[DL1])
    to_tiles(nn(matrix(inbox.at[L1]), matrix(inbox.at[DX1])), outbox.at[DR1])
    scatter(DR1, outbox.at[DR1], inbox.at[DR1])
    from_cells(POUT, cells_out.at[0], pair_out, quarters[1])

    def side_back(u, n, at, value, sig, tile):
        s = sig[u, :, lanes(n)]
        back = load(tile, n) * mask(n) * s
        dp[2 * at * C : (2 * at + 1) * C, lanes(n)] = back.astype(bf16)
        back = back * value[u, :, lanes(n)] * (1.0 - s)
        dp[(2 * at + 1) * C : 2 * (at + 1) * C, lanes(n)] = back.astype(bf16)

    def left_back(u, at):
        arrive(at, inbox.at[at])
        unpack(inbox.at[at], tile_a)

        @pl.loop(0, chunks)
        def _(n):
            side_back(u, n, 0, value_l, sig_l, tile_a)
            part[:, lanes(n)] = nn(wn[u, :, : 2 * C], dp[: 2 * C, lanes(n)]) + nn(
                wn[u, :, 4 * C :], dp[4 * C :, lanes(n)]
            )

    def prepare_back(u, n):
        right = nn(wn[u, :, 2 * C : 4 * C], dp[2 * C : 4 * C, lanes(n)])
        return norm_back(
            part[:, lanes(n)] + right, zhat[u, :, lanes(n)].astype(f32), zscale[u, :, lanes(n)]
        )

    left_back(1, DL1)
    arrive(DR1, inbox.at[DR1])
    unpack(inbox.at[DR1], tile_b)

    @pl.loop(0, chunks)
    def _(n):
        side_back(1, n, 1, value_r, sig_r, tile_b)
        cotangent = (load(tile_g, n) + prepare_back(1, n)).astype(bf16).astype(f32)
        dz[:, lanes(n)] = cotangent
        back = finish_back(0, n, cotangent)
        store(tile_a, n, norm_back(back, xhat[0, :, lanes(n)].astype(f32), xscale[:, lanes(n)]))

    pack(tile_a, outbox.at[DX0])
    scatter(DX0, outbox.at[DX0], inbox.at[DX0])

    from_cells(POUT, cells_out.at[0], pair_out, quarters[2])

    def lay(at, value):
        for t in range(value.shape[1] // C):
            tile_s[pl.ds(at + t, C, stride=SUM_ROWS), :] = value[:, t * C : (t + 1) * C]

    lay(AT_IN[1], nt(zhat[1], dp[...]))
    lay(AT_OUT[1], nt(xhat[1], du[1]))
    lay(AT_OUT[0], nt(xhat[0], du[0]))

    @pl.loop(0, chunks)
    def _(n):
        gate_back(0, n, dz[:, lanes(n)], upd[:, lanes(n)])

    lay(AT_IN[0] + 4, nt(zhat[0], dp[4 * C :]))
    for t in range(12, SUM_ROWS):
        lay(t, jnp.zeros((C, C), f32))

    arrive(DX0, inbox.at[DX0])
    to_tiles(nn(matrix(inbox.at[DX0]), matrix(inbox.at[R0])), outbox.at[DL0])
    scatter(DL0, outbox.at[DL0], inbox.at[DL0])
    to_tiles(tn(matrix(inbox.at[DX0]), matrix(inbox.at[L0])), outbox.at[DR0])
    scatter(DR0, outbox.at[DR0], inbox.at[DR0])
    from_cells(POUT, cells_out.at[0], pair_out, quarters[3])

    left_back(0, DL0)
    lay(AT_IN[0], nt(zhat[0], dp[: 2 * C]))
    arrive(DR0, inbox.at[DR0])
    unpack(inbox.at[DR0], tile_b)

    @pl.loop(0, chunks)
    def _(n):
        side_back(0, n, 1, value_r, sig_r, tile_b)

    lay(AT_IN[0] + 2, nt(zhat[0], dp[2 * C : 4 * C]))
    half = chips // 8

    @pl.loop(0, 8)
    def _(n):
        first = pl.multiple_of(n * block * SUM_ROWS, block * SUM_ROWS)
        some = tile_s[pl.ds(first, block * SUM_ROWS), :]
        sums[pl.ds(n * half, half)] = some.reshape(half, 2, SUM_ROWS, C).astype(bf16)

    to_sibling(CORES, sums.at[:, 1 - core], sums_core).start()

    @pl.loop(0, chunks)
    def _(n):
        store(tile_a, n, dz[:, lanes(n)] + prepare_back(0, n))

    to_sibling(CORES, sums.at[:, 1 - core], sums_core).wait_recv()

    @pl.loop(0, 8)
    def _(n):
        some = pl.ds(n * half, half)
        sums_chip[some] = (sums[some, core].astype(f32) + sums_core[some].astype(f32)).astype(bf16)

    over_chips(SCATTER, lambda other: sums_chip.at[other], sums_in.at[chip])
    pltpu.make_async_copy(sums_chip.at[chip], sums_in.at[chip], own.at[SCATTER]).start()
    pack(tile_a, cells_out.at[1])
    from_cells(GOUT, cells_out.at[1], grad_pair, every)

    pltpu.make_async_copy(sums_chip.at[chip], sums_in.at[chip], own.at[SCATTER]).wait()
    landed_chips(SCATTER).wait_recv()
    total[...] = jnp.sum(sums_in[...].astype(f32), axis=0).astype(bf16)
    over_chips(GATHER, lambda other: total, totals.at[core, chip])
    pltpu.make_async_copy(total, totals.at[core, chip], own.at[GATHER]).start()
    pltpu.make_async_copy(total, totals.at[core, chip], own.at[GATHER]).wait()
    landed_chips(GATHER).wait_recv()
    share = to_sibling(SHARE, totals.at[core], totals.at[core])
    share.start()
    share.wait_recv()

    @pl.loop(0, 8)
    def _(n):
        some = pl.ds(n * half, half)
        both = jnp.stack([totals[0, some], totals[1, some]], axis=1).astype(f32)
        first = pl.multiple_of(n * block * SUM_ROWS, block * SUM_ROWS)
        tile_s[pl.ds(first, block * SUM_ROWS), :] = both.reshape(block * SUM_ROWS, C)

    factor = 1.0 / (J * across)
    for u in range(2):
        for at, weights, gain, d_weights, d_gain in (
            (AT_IN[u], w_in, gain_in, d_w_in, d_gain_in),
            (AT_OUT[u], w_out, gain_mid, d_w_out, d_gain_mid),
        ):
            column = jnp.transpose(jnp.broadcast_to(gain[pl.ds(u, 1), :] * factor, (C, C)))
            both = jnp.zeros((C, C), f32)
            for t in range(weights.shape[2] // C):
                part = slice(t * C, (t + 1) * C)
                rows_sum = tile_s[pl.ds(at + t, C, stride=SUM_ROWS), :]
                d_weights[u, :, part] = rows_sum * column
                both = both + rows_sum * weights[u, :, part].astype(f32)
            d_gain[pl.ds(u, 1), :] = jnp.sum(jnp.transpose(both), axis=0, keepdims=True) * factor

    arrive_chan(POUT, cells_out.at[0])
    arrive_chan(GOUT, cells_out.at[1])
    for at in range(12):
        landed(at, outbox.at[at]).wait_send()
    for at in range(PAIR, GOUT + 1):
        landed_chan(at, cells_out.at[0]).wait_send()
    to_sibling(CORES, sums.at[:, 1 - core], sums_core).wait_send()
    landed_chips(SCATTER).wait_send()
    landed_chips(GATHER).wait_send()
    share.wait_send()


def local(groups, pair, grad_out, residue_chain, gain_in, w_in, gain_mid, w_out):
    C = w_in.shape[1]
    own_c, own_rows, size = pair.shape
    devices = C
    across = 4 if groups == 16 else 2
    J = size // across
    rows = own_rows * across // groups
    cells = rows * J
    dims = (C, rows, J, groups, across, devices)
    whole = pl.BlockSpec(memory_space=pltpu.VMEM)
    far = pl.BlockSpec(memory_space=pl.ANY)
    box = (C, rows, J)
    return pl.pallas_call(
        partial(kernel, dims),
        out_shape=[
            jax.ShapeDtypeStruct(pair.shape, bf16),
            jax.ShapeDtypeStruct(pair.shape, bf16),
            jax.ShapeDtypeStruct(gain_in.shape, f32),
            jax.ShapeDtypeStruct(w_in.shape, f32),
            jax.ShapeDtypeStruct(gain_mid.shape, f32),
            jax.ShapeDtypeStruct(w_out.shape, f32),
        ],
        in_specs=[far, far, pl.BlockSpec(memory_space=pltpu.SMEM)] + [whole] * 5,
        out_specs=[far, far] + [whole] * 4,
        scratch_shapes=[
            pltpu.VMEM((12,) + box, bf16),
            pltpu.VMEM((12,) + box, bf16),
            pltpu.VMEM((2,) + box, bf16),
            pltpu.VMEM((2,) + box, bf16),
            pltpu.VMEM((C // 2, 2, SUM_ROWS, C), bf16),
            pltpu.VMEM((C // 2, SUM_ROWS, C), bf16),
            pltpu.VMEM((C // 2, SUM_ROWS, C), bf16),
            pltpu.VMEM((C // 2, SUM_ROWS, C), bf16),
            pltpu.VMEM((SUM_ROWS, C), bf16),
            pltpu.VMEM((2, C // 2, SUM_ROWS, C), bf16),
            pltpu.VMEM((C * SUM_ROWS, C), f32),
            pltpu.VMEM((2, 5 * C, C), bf16),
            pltpu.VMEM((2, C, 5 * C), bf16),
            pltpu.VMEM((2, C, C), bf16),
            pltpu.VMEM((2, C, C), bf16),
            pltpu.VMEM((C * rows, J), f32),
            pltpu.VMEM((C * rows, J), f32),
            pltpu.VMEM((C * rows, J), f32),
            pltpu.VMEM((2, C, cells), f32),
            pltpu.VMEM((2, C, cells), bf16),
            pltpu.VMEM((2, 1, cells), f32),
            pltpu.VMEM((2, C, cells), bf16),
            pltpu.VMEM((1, cells), f32),
            pltpu.VMEM((2, C, cells), f32),
            pltpu.VMEM((2, C, cells), f32),
            pltpu.VMEM((2, C, cells), f32),
            pltpu.VMEM((2, C, cells), f32),
            pltpu.VMEM((2, C, cells), f32),
            pltpu.VMEM((C, cells), f32),
            pltpu.VMEM((2, C, cells), bf16),
            pltpu.VMEM((C, cells), f32),
            pltpu.VMEM((5 * C, cells), bf16),
            pltpu.VMEM((C, cells), f32),
            pltpu.SemaphoreType.DMA((EXCHANGES,)),
            pltpu.SemaphoreType.DMA((EXCHANGES,)),
            pltpu.SemaphoreType.DMA((EXCHANGES,)),
        ],
        compiler_params=pltpu.CompilerParams(
            collective_id=0, has_side_effects=True, vmem_limit_bytes=60 * 2**20
        ),
    )(
        pair,
        grad_out,
        residue_chain,
        residue_chain.reshape(across, J),
        w_in,
        w_out,
        gain_in,
        gain_mid,
    )


def solution(mesh):
    return jax.shard_map(
        partial(local, mesh.shape["chan"]),
        mesh=mesh,
        in_specs=(P("chan", "row", None), P("chan", "row", None), P(), P(), P(), P(), P()),
        out_specs=(P("chan", "row", None), P("chan", "row", None), P(), P(), P(), P()),
        check_vma=False,
    )
```

```python
from functools import partial

import jax
import jax.numpy as jnp
from jax import lax
from jax.experimental import pallas as pl
from jax.experimental.pallas import tpu as pltpu
from jax.sharding import PartitionSpec as P

epsilon = 1e-05
MESH = pl.DeviceIdType.MESH
f32 = jnp.float32
bf16 = jnp.bfloat16

L0, R0, X0, L1, R1, X1, DX1, DL1, DR1, DX0, DL0, DR0 = range(12)
PAIR, GRAD, POUT, GOUT = range(12, 16)
CORES, SCATTER, GATHER, SHARE = range(16, 20)
LATE_CHAN, LATE_ROW, LATE_ALL = range(20, 23)
EXCHANGES = 23
AT_IN1, AT_OUT, AT_GATE0 = 0, (6, 5), 7
SUM_ROWS = 8
LATE_ROWS = 4


def nn(a, b):
    return lax.dot_general(a, b, (((1,), (0,)), ((), ())), preferred_element_type=f32)


def nt(a, b):
    return lax.dot_general(a, b, (((1,), (1,)), ((), ())), preferred_element_type=f32)


def tn(a, b):
    return lax.dot_general(a, b, (((0,), (0,)), ((), ())), preferred_element_type=f32)


def sigmoid(x):
    return 0.5 * jnp.tanh(0.5 * x) + 0.5


def norm(z):
    center = z - jnp.mean(z, axis=0, keepdims=True)
    scale = lax.rsqrt(jnp.mean(center * center, axis=0, keepdims=True) + epsilon)
    return center * scale, scale


def norm_back(grad, normed, scale):
    mean_grad = jnp.mean(grad, axis=0, keepdims=True)
    mean_both = jnp.mean(grad * normed, axis=0, keepdims=True)
    return scale * (grad - mean_grad - normed * mean_both)


def kernel(
    dims,
    pair,
    grad,
    chain_s,
    chain_far,
    w_in_far,
    w_out_far,
    gain_in_far,
    gain_mid_far,
    pair_out,
    grad_pair,
    d_gain_in,
    d_w_in,
    d_gain_mid,
    d_w_out,
    chain_v,
    w_in,
    w_out,
    gain_in,
    gain_mid,
    outbox,
    inbox,
    cells_out,
    cells_in,
    sums,
    sums_core,
    sums_chip,
    sums_in,
    total,
    totals,
    tile_s,
    late,
    late_out,
    late_in,
    late_part,
    late_rows,
    late_sum,
    late_all,
    columns_g,
    wt,
    wn,
    wot,
    won,
    tile_a,
    tile_b,
    tile_g,
    field,
    zhat,
    zscale,
    xhat,
    xscale,
    value_l,
    sig_l,
    value_r,
    sig_r,
    gate,
    upd,
    du,
    part,
    dp,
    dz,
    send,
    recv,
    own,
    fetched,
):
    C, rows, J, groups, across, devices = dims
    per = 16
    chunks = rows // per
    wide = per * J
    row, chan = lax.axis_index("row"), lax.axis_index("chan")
    me = row * groups + chan
    tile_i, tile_j = chan // across, lax.rem(chan, across)

    def place(to):
        return (to // groups, lax.rem(to, groups))

    small = [
        pltpu.make_async_copy(src, dst, fetched.at[n])
        for n, (src, dst) in enumerate(
            (
                (chain_far, chain_v),
                (w_in_far, w_in),
                (w_out_far, w_out),
                (gain_in_far, gain_in),
                (gain_mid_far, gain_mid),
            )
        )
    ]
    for copy in small:
        copy.start()
    barrier = pltpu.get_barrier_semaphore()

    def greet(step, carry):
        other = lax.rem(me + step, devices)
        pl.semaphore_signal(barrier, inc=1, device_id=place(other), device_id_type=MESH)
        return carry

    lax.fori_loop(1, devices, greet, 0)
    pl.semaphore_wait(barrier, devices - 1)

    def scatter(at, src, dst):
        def step(k, carry):
            other = lax.rem(me + k, devices)
            pltpu.make_async_remote_copy(
                src_ref=src.at[other],
                dst_ref=dst.at[me],
                send_sem=send.at[at],
                recv_sem=recv.at[at],
                device_id=place(other),
                device_id_type=MESH,
            ).start()
            return carry

        lax.fori_loop(1, devices, step, 0)
        pltpu.make_async_copy(src.at[me], dst.at[me], own.at[at]).start()

    chips, core = devices // 2, lax.rem(me, 2)
    chip = me // 2

    def over_chips(at, source, dst):
        def step(k, carry):
            other = lax.rem(chip + k, chips)
            pltpu.make_async_remote_copy(
                src_ref=source(other),
                dst_ref=dst,
                send_sem=send.at[at],
                recv_sem=recv.at[at],
                device_id=place(2 * other + core),
                device_id_type=MESH,
            ).start()
            return carry

        lax.fori_loop(1, chips, step, 0)

    def to_sibling(at, src, dst):
        return pltpu.make_async_remote_copy(
            src_ref=src,
            dst_ref=dst,
            send_sem=send.at[at],
            recv_sem=recv.at[at],
            device_id=place(2 * chip + 1 - core),
            device_id_type=MESH,
        )

    def over_chan(at, source, dst):
        def step(k, carry):
            other = lax.rem(chan + k, groups)
            pltpu.make_async_remote_copy(
                src_ref=source(other),
                dst_ref=dst.at[chan],
                send_sem=send.at[at],
                recv_sem=recv.at[at],
                device_id=(row, other),
                device_id_type=MESH,
            ).start()
            return carry

        lax.fori_loop(1, groups, step, 0)
        pltpu.make_async_copy(source(chan), dst.at[chan], own.at[at]).start()

    def over_rows(at, src, dst):
        def step(k, carry):
            other = lax.rem(row + k, devices // groups)
            pltpu.make_async_remote_copy(
                src_ref=src,
                dst_ref=dst.at[row],
                send_sem=send.at[at],
                recv_sem=recv.at[at],
                device_id=(other, chan),
                device_id_type=MESH,
            ).start()
            return carry

        lax.fori_loop(1, devices // groups, step, 0)
        pltpu.make_async_copy(src, dst.at[row], own.at[at]).start()

    def landed_late(at, like):
        rest = like.at[pl.ds(0, like.shape[0] - 1)]
        return to_sibling(at, rest, rest)

    def arrive_late(at, like):
        pltpu.make_async_copy(like.at[0], like.at[0], own.at[at]).wait()
        landed_late(at, like).wait_recv()

    def landed_chips(at):
        rest = sums_in.at[pl.ds(0, chips - 1)]
        return to_sibling(at, rest, rest)

    def landed(at, like):
        rest = like.at[pl.ds(0, devices - 1)]
        return pltpu.make_async_remote_copy(
            src_ref=rest,
            dst_ref=rest,
            send_sem=send.at[at],
            recv_sem=recv.at[at],
            device_id=(row, chan),
            device_id_type=MESH,
        )

    def arrive(at, like):
        pltpu.make_async_copy(like.at[0], like.at[0], own.at[at]).wait()
        landed(at, like).wait_recv()

    own_c = C // groups
    every = (0, groups)
    quarters = [(q * groups // 4, (q + 1) * groups // 4) for q in range(4)]

    def tile_of(ref, other):
        first = pl.multiple_of((other // across) * rows, rows)
        left = pl.multiple_of(lax.rem(other, across) * J, J)
        return ref.at[:, pl.ds(first, rows), pl.ds(left, J)]

    def channels(ref, other):
        return ref.at[pl.ds(pl.multiple_of(other * own_c, own_c), own_c)]

    def to_cells(at, src, dst, piece):
        def step(k, carry):
            other = lax.rem(chan + k, groups)
            pltpu.make_async_remote_copy(
                src_ref=tile_of(src, other),
                dst_ref=channels(dst, chan),
                send_sem=send.at[at],
                recv_sem=recv.at[at],
                device_id=(row, other),
                device_id_type=MESH,
            ).start()
            return carry

        lax.fori_loop(max(1, piece[0]), piece[1], step, 0)
        if piece[0] == 0:
            pltpu.make_async_copy(tile_of(src, chan), channels(dst, chan), own.at[at]).start()

    def from_cells(at, src, dst, piece):
        def step(k, carry):
            other = lax.rem(chan + k, groups)
            pltpu.make_async_remote_copy(
                src_ref=channels(src, other),
                dst_ref=tile_of(dst, chan),
                send_sem=send.at[at],
                recv_sem=recv.at[at],
                device_id=(row, other),
                device_id_type=MESH,
            ).start()
            return carry

        lax.fori_loop(max(1, piece[0]), piece[1], step, 0)
        if piece[0] == 0:
            pltpu.make_async_copy(channels(src, chan), tile_of(dst, chan), own.at[at]).start()

    def landed_chan(at, like):
        rest = like.at[pl.ds(0, C - own_c)]
        return pltpu.make_async_remote_copy(
            src_ref=rest,
            dst_ref=rest,
            send_sem=send.at[at],
            recv_sem=recv.at[at],
            device_id=(row, chan),
            device_id_type=MESH,
        )

    def arrive_chan(at, like):
        part = like.at[pl.ds(0, own_c)]
        pltpu.make_async_copy(part, part, own.at[at]).wait()
        landed_chan(at, like).wait_recv()

    block = C // 8

    def unpack(box, tile):
        @pl.loop(0, 8)
        def _(n):
            some = box[pl.ds(n * block, block)].astype(f32)
            first = pl.multiple_of(n * block * rows, block * rows)
            tile[pl.ds(first, block * rows), :] = some.reshape(block * rows, J)

    def pack(tile, box):
        @pl.loop(0, 8)
        def _(n):
            first = pl.multiple_of(n * block * rows, block * rows)
            some = tile[pl.ds(first, block * rows), :]
            box[pl.ds(n * block, block)] = some.reshape(block, rows, J).astype(bf16)

    def load(tile, n):
        return jnp.concatenate(
            [tile[pl.ds(n * per + s, C, stride=rows), :] for s in range(per)], axis=1
        )

    def store(tile, n, value):
        for s in range(per):
            tile[pl.ds(n * per + s, C, stride=rows), :] = value[:, s * J : (s + 1) * J]

    def lanes(n):
        return pl.ds(pl.multiple_of(n * wide, wide), wide)

    first_row = row * (rows * groups // across) + tile_i * rows

    def mask(n):
        columns = (chain_v[pl.ds(tile_j, 1), :] > 0).astype(f32)
        return jnp.concatenate(
            [
                columns * (chain_s[first_row + n * per + s] > 0).astype(f32)
                for s in range(per)
            ],
            axis=1,
        )

    def matrix(box):
        high = devices // across
        tiles = box[...].reshape(high, across, rows, J)
        return jnp.concatenate(
            [tiles[:, t].reshape(high * rows, J) for t in range(across)], axis=1
        )

    def to_tiles(value, box):
        high = devices // across
        value = value.astype(bf16)
        for i in range(high):
            for t in range(across):
                box[i * across + t] = value[i * rows : (i + 1) * rows, t * J : (t + 1) * J]

    to_cells(PAIR, pair, cells_in.at[0], every)
    to_cells(GRAD, grad, cells_in.at[1], quarters[0])
    for copy in small:
        copy.wait()
    for u in range(2):
        turned = jnp.transpose(w_in[u].astype(f32)) * gain_in[pl.ds(u, 1), :]
        wt[u] = turned.astype(bf16)
        wn[u] = jnp.transpose(turned).astype(bf16)
        turned = jnp.transpose(w_out[u].astype(f32)) * gain_mid[pl.ds(u, 1), :]
        wot[u] = turned.astype(bf16)
        won[u] = jnp.transpose(turned).astype(bf16)
        for at, gain in ((u, gain_in), (2 + u, gain_mid)):
            scaled = gain[pl.ds(u, 1), :] * (1.0 / (J * across))
            columns_g[at] = jnp.transpose(jnp.broadcast_to(scaled, (C, C)))

    def side(u, n, at, value, sig, tile):
        p = nn(wt[u, 2 * at * C : 2 * (at + 1) * C, :], zhat[u, :, lanes(n)])
        v, s = p[:C], sigmoid(p[C:])
        value[u, :, lanes(n)] = v
        sig[u, :, lanes(n)] = s
        store(tile, n, mask(n) * s * v)

    def prepare(u, at_l, at_r):
        pack(tile_a, outbox.at[at_l])
        scatter(at_l, outbox.at[at_l], inbox.at[at_l])

        @pl.loop(0, chunks)
        def _(n):
            side(u, n, 1, value_r, sig_r, tile_b)

        pack(tile_b, outbox.at[at_r])
        scatter(at_r, outbox.at[at_r], inbox.at[at_r])

        @pl.loop(0, chunks)
        def _(n):
            p = nn(wt[u, 4 * C :, :], zhat[u, :, lanes(n)])
            gate[u, :, lanes(n)] = sigmoid(p).astype(bf16).astype(f32)

    arrive_chan(PAIR, cells_in.at[0])
    unpack(cells_in.at[0], tile_b)

    @pl.loop(0, chunks)
    def _(n):
        z = load(tile_b, n)
        field[0, :, lanes(n)] = z
        normed, scale = norm(z)
        zhat[0, :, lanes(n)] = normed.astype(bf16)
        zscale[0, :, lanes(n)] = scale
        side(0, n, 0, value_l, sig_l, tile_a)

    prepare(0, L0, R0)
    to_cells(GRAD, grad, cells_in.at[1], quarters[1])
    arrive(L0, inbox.at[L0])
    arrive(R0, inbox.at[R0])
    to_tiles(nt(matrix(inbox.at[L0]), matrix(inbox.at[R0])), outbox.at[X0])
    scatter(X0, outbox.at[X0], inbox.at[X0])
    to_cells(GRAD, grad, cells_in.at[1], quarters[2])

    arrive(X0, inbox.at[X0])
    unpack(inbox.at[X0], tile_b)

    @pl.loop(0, chunks)
    def _(n):
        normed, scale = norm(load(tile_b, n))
        normed = normed.astype(bf16)
        xhat[0, :, lanes(n)] = normed
        xscale[:, lanes(n)] = scale
        update = nn(wot[0], normed)
        upd[:, lanes(n)] = update
        z = (field[0, :, lanes(n)] + gate[0, :, lanes(n)] * update).astype(bf16).astype(f32)
        field[1, :, lanes(n)] = z
        normed, scale = norm(z)
        zhat[1, :, lanes(n)] = normed.astype(bf16)
        zscale[1, :, lanes(n)] = scale
        side(1, n, 0, value_l, sig_l, tile_a)

    prepare(1, L1, R1)
    to_cells(GRAD, grad, cells_in.at[1], quarters[3])
    arrive(L1, inbox.at[L1])
    arrive(R1, inbox.at[R1])
    to_tiles(tn(matrix(inbox.at[L1]), matrix(inbox.at[R1])), outbox.at[X1])
    scatter(X1, outbox.at[X1], inbox.at[X1])
    arrive_chan(GRAD, cells_in.at[1])
    unpack(cells_in.at[1], tile_g)

    def finish_back(u, n, cotangent):
        back = (cotangent * gate[u, :, lanes(n)]).astype(bf16)
        du[u, :, lanes(n)] = back
        return nn(won[u], back)

    @pl.loop(0, chunks)
    def _(n):
        part[:, lanes(n)] = finish_back(1, n, load(tile_g, n))

    arrive(X1, inbox.at[X1])
    unpack(inbox.at[X1], tile_b)

    @pl.loop(0, chunks)
    def _(n):
        normed, scale = norm(load(tile_b, n))
        xhat[1, :, lanes(n)] = normed.astype(bf16)
        store(tile_a, n, norm_back(part[:, lanes(n)], normed, scale))

    pack(tile_a, outbox.at[DX1])
    scatter(DX1, outbox.at[DX1], inbox.at[DX1])

    def gate_back(u, n, cotangent, update):
        s = gate[u, :, lanes(n)]
        back = (cotangent * update).astype(bf16).astype(f32)
        dp[4 * C :, lanes(n)] = (back * s * (1.0 - s)).astype(bf16)

    @pl.loop(0, chunks)
    def _(n):
        update = nn(wot[1], xhat[1, :, lanes(n)])
        store(tile_b, n, field[1, :, lanes(n)] + gate[1, :, lanes(n)] * update)
        gate_back(1, n, load(tile_g, n), update)

    pack(tile_b, cells_out.at[0])
    from_cells(POUT, cells_out.at[0], pair_out, quarters[0])

    arrive(DX1, inbox.at[DX1])
    to_tiles(nt(matrix(inbox.at[R1]), matrix(inbox.at[DX1])), outbox.at[DL1])
    scatter(DL1, outbox.at[DL1], inbox.at[DL1])
    to_tiles(nn(matrix(inbox.at[L1]), matrix(inbox.at[DX1])), outbox.at[DR1])
    scatter(DR1, outbox.at[DR1], inbox.at[DR1])
    from_cells(POUT, cells_out.at[0], pair_out, quarters[1])

    def side_back(u, n, at, value, sig, tile):
        s = sig[u, :, lanes(n)]
        back = load(tile, n) * mask(n) * s
        dp[2 * at * C : (2 * at + 1) * C, lanes(n)] = back.astype(bf16)
        back = back * value[u, :, lanes(n)] * (1.0 - s)
        dp[(2 * at + 1) * C : 2 * (at + 1) * C, lanes(n)] = back.astype(bf16)

    def left_back(u, at):
        arrive(at, inbox.at[at])
        unpack(inbox.at[at], tile_a)

        @pl.loop(0, chunks)
        def _(n):
            side_back(u, n, 0, value_l, sig_l, tile_a)
            part[:, lanes(n)] = nn(wn[u, :, : 2 * C], dp[: 2 * C, lanes(n)]) + nn(
                wn[u, :, 4 * C :], dp[4 * C :, lanes(n)]
            )

    def prepare_back(u, n):
        right = nn(wn[u, :, 2 * C : 4 * C], dp[2 * C : 4 * C, lanes(n)])
        return norm_back(
            part[:, lanes(n)] + right, zhat[u, :, lanes(n)].astype(f32), zscale[u, :, lanes(n)]
        )

    left_back(1, DL1)
    arrive(DR1, inbox.at[DR1])
    unpack(inbox.at[DR1], tile_b)

    @pl.loop(0, chunks)
    def _(n):
        side_back(1, n, 1, value_r, sig_r, tile_b)
        cotangent = (load(tile_g, n) + prepare_back(1, n)).astype(bf16).astype(f32)
        dz[:, lanes(n)] = cotangent
        back = finish_back(0, n, cotangent)
        store(tile_a, n, norm_back(back, xhat[0, :, lanes(n)].astype(f32), xscale[:, lanes(n)]))

    pack(tile_a, outbox.at[DX0])
    scatter(DX0, outbox.at[DX0], inbox.at[DX0])

    from_cells(POUT, cells_out.at[0], pair_out, quarters[2])

    def lay(at, value):
        for t in range(value.shape[1] // C):
            tile_s[pl.ds(at + t, C, stride=SUM_ROWS), :] = value[:, t * C : (t + 1) * C]

    lay(AT_IN1, nt(zhat[1], dp[...]))
    lay(AT_OUT[1], nt(xhat[1], du[1]))
    lay(AT_OUT[0], nt(xhat[0], du[0]))

    @pl.loop(0, chunks)
    def _(n):
        gate_back(0, n, dz[:, lanes(n)], upd[:, lanes(n)])

    lay(AT_GATE0, nt(zhat[0], dp[4 * C :]))
    half = chips // 8

    @pl.loop(0, 8)
    def _(n):
        first = pl.multiple_of(n * block * SUM_ROWS, block * SUM_ROWS)
        some = tile_s[pl.ds(first, block * SUM_ROWS), :]
        sums[pl.ds(n * half, half)] = some.reshape(half, 2, SUM_ROWS, C)

    to_sibling(CORES, sums.at[:, 1 - core], sums_core).start()
    to_sibling(CORES, sums.at[:, 1 - core], sums_core).wait_recv()

    @pl.loop(0, 8)
    def _(n):
        some = pl.ds(n * half, half)
        sums_chip[some] = sums[some, core] + sums_core[some]

    over_chips(SCATTER, lambda other: sums_chip.at[other], sums_in.at[chip])
    pltpu.make_async_copy(sums_chip.at[chip], sums_in.at[chip], own.at[SCATTER]).start()

    arrive(DX0, inbox.at[DX0])
    to_tiles(nn(matrix(inbox.at[DX0]), matrix(inbox.at[R0])), outbox.at[DL0])
    scatter(DL0, outbox.at[DL0], inbox.at[DL0])
    to_tiles(tn(matrix(inbox.at[DX0]), matrix(inbox.at[L0])), outbox.at[DR0])
    scatter(DR0, outbox.at[DR0], inbox.at[DR0])
    pltpu.make_async_copy(sums_chip.at[chip], sums_in.at[chip], own.at[SCATTER]).wait()
    landed_chips(SCATTER).wait_recv()
    total[...] = jnp.sum(sums_in[...], axis=0)
    over_chips(GATHER, lambda other: total, totals.at[core, chip])
    pltpu.make_async_copy(total, totals.at[core, chip], own.at[GATHER]).start()
    from_cells(POUT, cells_out.at[0], pair_out, quarters[3])

    left_back(0, DL0)

    def lay_late(at, value):
        for t in range(value.shape[1] // C):
            late[pl.ds(at + t, C, stride=LATE_ROWS), :] = value[:, t * C : (t + 1) * C]

    lay_late(0, nt(zhat[0], dp[: 2 * C]))
    arrive(DR0, inbox.at[DR0])
    unpack(inbox.at[DR0], tile_b)

    @pl.loop(0, chunks)
    def _(n):
        side_back(0, n, 1, value_r, sig_r, tile_b)

    lay_late(2, nt(zhat[0], dp[2 * C : 4 * C]))
    late_out[...] = late[...].reshape(late_out.shape).astype(bf16)
    over_chan(LATE_CHAN, lambda other: late_out.at[other], late_in)
    pltpu.make_async_copy(total, totals.at[core, chip], own.at[GATHER]).wait()
    landed_chips(GATHER).wait_recv()
    share = to_sibling(SHARE, totals.at[core], totals.at[core])
    share.start()

    @pl.loop(0, chunks)
    def _(n):
        store(tile_a, n, dz[:, lanes(n)] + prepare_back(0, n))

    pack(tile_a, cells_out.at[1])
    from_cells(GOUT, cells_out.at[1], grad_pair, (0, groups // 2))

    arrive_late(LATE_CHAN, late_in)
    late_part[...] = jnp.sum(late_in[...].astype(f32), axis=0).astype(bf16)
    over_rows(LATE_ROW, late_part, late_rows)
    from_cells(GOUT, cells_out.at[1], grad_pair, (groups // 2, groups))
    share.wait_recv()

    @pl.loop(0, 8)
    def _(n):
        some = pl.ds(n * half, half)
        both = jnp.stack([totals[0, some], totals[1, some]], axis=1)
        first = pl.multiple_of(n * block * SUM_ROWS, block * SUM_ROWS)
        tile_s[pl.ds(first, block * SUM_ROWS), :] = both.reshape(block * SUM_ROWS, C)

    def put(u, at, weights, d_weights, d_gain, fetch):
        both = jnp.zeros((C, C), f32)
        for t in range(weights.shape[2] // C):
            columns_t = slice(t * C, (t + 1) * C)
            rows_sum = fetch(t)
            d_weights[u, :, columns_t] = rows_sum * columns_g[at]
            both = both + rows_sum * weights[u, :, columns_t].astype(f32)
        row_sum = jnp.sum(jnp.transpose(both), axis=0, keepdims=True)
        d_gain[pl.ds(u, 1), :] = row_sum * (1.0 / (J * across))

    def early(at):
        return tile_s[pl.ds(at, C, stride=SUM_ROWS), :]

    def last(t):
        return late[pl.ds(t, C, stride=LATE_ROWS), :] if t < LATE_ROWS else early(AT_GATE0)

    arrive_late(LATE_ROW, late_rows)
    late_sum[...] = jnp.sum(late_rows[...].astype(f32), axis=0).astype(bf16)
    over_chan(LATE_ALL, lambda other: late_sum, late_all)
    put(1, 1, w_in, d_w_in, d_gain_in, lambda t: early(AT_IN1 + t))
    put(0, 2, w_out, d_w_out, d_gain_mid, lambda t: early(AT_OUT[0]))
    put(1, 3, w_out, d_w_out, d_gain_mid, lambda t: early(AT_OUT[1]))

    arrive_late(LATE_ALL, late_all)
    late[...] = late_all[...].astype(f32).reshape(late.shape)
    put(0, 0, w_in, d_w_in, d_gain_in, last)

    arrive_chan(POUT, cells_out.at[0])
    arrive_chan(GOUT, cells_out.at[1])
    for at in range(12):
        landed(at, outbox.at[at]).wait_send()
    for at in range(PAIR, GOUT + 1):
        landed_chan(at, cells_out.at[0]).wait_send()
    to_sibling(CORES, sums.at[:, 1 - core], sums_core).wait_send()
    landed_chips(SCATTER).wait_send()
    landed_chips(GATHER).wait_send()
    share.wait_send()
    landed_late(LATE_CHAN, late_in).wait_send()
    landed_late(LATE_ROW, late_rows).wait_send()
    landed_late(LATE_ALL, late_all).wait_send()


def hand_on(*refs):
    count = len(refs) // 2
    for got, out in zip(refs[:count], refs[count:]):
        out[...] = got[...]


def local(groups, pair, grad_out, residue_chain, gain_in, w_in, gain_mid, w_out):
    C = w_in.shape[1]
    own_c, own_rows, size = pair.shape
    devices = C
    across = 4 if groups == 16 else 2
    J = size // across
    rows = own_rows * across // groups
    cells = rows * J
    dims = (C, rows, J, groups, across, devices)
    whole = pl.BlockSpec(memory_space=pltpu.VMEM)
    far = pl.BlockSpec(memory_space=pl.ANY)
    box = (C, rows, J)
    late_rows = C // groups * LATE_ROWS
    got = pl.pallas_call(
        partial(kernel, dims),
        out_shape=[
            jax.ShapeDtypeStruct(pair.shape, bf16),
            jax.ShapeDtypeStruct(pair.shape, bf16),
            jax.ShapeDtypeStruct(gain_in.shape, f32),
            jax.ShapeDtypeStruct(w_in.shape, f32),
            jax.ShapeDtypeStruct(gain_mid.shape, f32),
            jax.ShapeDtypeStruct(w_out.shape, f32),
        ],
        in_specs=[far, far, pl.BlockSpec(memory_space=pltpu.SMEM)] + [far] * 5,
        out_specs=[whole] * 6,
        scratch_shapes=[
            pltpu.VMEM((across, J), jnp.int32),
            pltpu.VMEM(w_in.shape, bf16),
            pltpu.VMEM(w_out.shape, bf16),
            pltpu.VMEM(gain_in.shape, f32),
            pltpu.VMEM(gain_mid.shape, f32),
            pltpu.VMEM((12,) + box, bf16),
            pltpu.VMEM((12,) + box, bf16),
            pltpu.VMEM((2,) + box, bf16),
            pltpu.VMEM((2,) + box, bf16),
            pltpu.VMEM((C // 2, 2, SUM_ROWS, C), f32),
            pltpu.VMEM((C // 2, SUM_ROWS, C), f32),
            pltpu.VMEM((C // 2, SUM_ROWS, C), f32),
            pltpu.VMEM((C // 2, SUM_ROWS, C), f32),
            pltpu.VMEM((SUM_ROWS, C), f32),
            pltpu.VMEM((2, C // 2, SUM_ROWS, C), f32),
            pltpu.VMEM((C * SUM_ROWS, C), f32),
            pltpu.VMEM((C * LATE_ROWS, C), f32),
            pltpu.VMEM((groups, late_rows, C), bf16),
            pltpu.VMEM((groups, late_rows, C), bf16),
            pltpu.VMEM((late_rows, C), bf16),
            pltpu.VMEM((devices // groups, late_rows, C), bf16),
            pltpu.VMEM((late_rows, C), bf16),
            pltpu.VMEM((groups, late_rows, C), bf16),
            pltpu.VMEM((4, C, C), f32),
            pltpu.VMEM((2, 5 * C, C), bf16),
            pltpu.VMEM((2, C, 5 * C), bf16),
            pltpu.VMEM((2, C, C), bf16),
            pltpu.VMEM((2, C, C), bf16),
            pltpu.VMEM((C * rows, J), f32),
            pltpu.VMEM((C * rows, J), f32),
            pltpu.VMEM((C * rows, J), f32),
            pltpu.VMEM((2, C, cells), f32),
            pltpu.VMEM((2, C, cells), bf16),
            pltpu.VMEM((2, 1, cells), f32),
            pltpu.VMEM((2, C, cells), bf16),
            pltpu.VMEM((1, cells), f32),
            pltpu.VMEM((2, C, cells), f32),
            pltpu.VMEM((2, C, cells), f32),
            pltpu.VMEM((2, C, cells), f32),
            pltpu.VMEM((2, C, cells), f32),
            pltpu.VMEM((2, C, cells), f32),
            pltpu.VMEM((C, cells), f32),
            pltpu.VMEM((2, C, cells), bf16),
            pltpu.VMEM((C, cells), f32),
            pltpu.VMEM((5 * C, cells), bf16),
            pltpu.VMEM((C, cells), f32),
            pltpu.SemaphoreType.DMA((EXCHANGES,)),
            pltpu.SemaphoreType.DMA((EXCHANGES,)),
            pltpu.SemaphoreType.DMA((EXCHANGES,)),
            pltpu.SemaphoreType.DMA((5,)),
        ],
        compiler_params=pltpu.CompilerParams(
            collective_id=0, has_side_effects=True, vmem_limit_bytes=60 * 2**20
        ),
    )(
        pair,
        grad_out,
        residue_chain,
        residue_chain.reshape(across, J),
        w_in,
        w_out,
        gain_in,
        gain_mid,
    )
    return pl.pallas_call(
        hand_on,
        out_shape=[jax.ShapeDtypeStruct(g.shape, g.dtype) for g in got],
        in_specs=[whole] * len(got),
        out_specs=[whole] * len(got),
    )(*got)


def solution(mesh):
    return jax.shard_map(
        partial(local, mesh.shape["chan"]),
        mesh=mesh,
        in_specs=(P("chan", "row", None), P("chan", "row", None), P(), P(), P(), P(), P()),
        out_specs=(P("chan", "row", None), P("chan", "row", None), P(), P(), P(), P()),
        check_vma=False,
    )
```

```python
from functools import partial

import jax
import jax.numpy as jnp
from jax import lax
from jax.experimental import pallas as pl
from jax.experimental.pallas import tpu as pltpu
from jax.sharding import PartitionSpec as P

epsilon = 1e-05
MESH = pl.DeviceIdType.MESH
f32 = jnp.float32
bf16 = jnp.bfloat16

L0, R0, X0, L1, R1, X1, DX1, DL1, DR1, DX0, DL0, DR0 = range(12)
PAIR, GRAD, POUT, GOUT = range(12, 16)
CORES, SCATTER, GATHER, SHARE = range(16, 20)
LATE_CHAN, LATE_ROW, LATE_ALL = range(20, 23)
EXCHANGES = 23
AT_IN1, AT_OUT, AT_GATE0 = 0, (6, 5), 7
SUM_ROWS = 8
LATE_ROWS = 4


def nn(a, b):
    return lax.dot_general(a, b, (((1,), (0,)), ((), ())), preferred_element_type=f32)


def nt(a, b):
    return lax.dot_general(a, b, (((1,), (1,)), ((), ())), preferred_element_type=f32)


def tn(a, b):
    return lax.dot_general(a, b, (((0,), (0,)), ((), ())), preferred_element_type=f32)


def sigmoid(x):
    return 0.5 * jnp.tanh(0.5 * x) + 0.5


def norm(z):
    center = z - jnp.mean(z, axis=0, keepdims=True)
    scale = lax.rsqrt(jnp.mean(center * center, axis=0, keepdims=True) + epsilon)
    return center * scale, scale


def norm_back(grad, normed, scale):
    mean_grad = jnp.mean(grad, axis=0, keepdims=True)
    mean_both = jnp.mean(grad * normed, axis=0, keepdims=True)
    return scale * (grad - mean_grad - normed * mean_both)


def kernel(
    dims,
    pair,
    grad,
    chain_s,
    chain_far,
    w_in_far,
    w_out_far,
    gain_in_far,
    gain_mid_far,
    pair_out,
    grad_pair,
    d_gain_in,
    d_w_in,
    d_gain_mid,
    d_w_out,
    chain_v,
    w_in,
    w_out,
    gain_in,
    gain_mid,
    outbox,
    inbox,
    cells_out,
    cells_in,
    sums,
    sums_core,
    sums_chip,
    sums_in,
    total,
    totals,
    tile_s,
    late,
    late_out,
    late_in,
    late_part,
    late_rows,
    late_sum,
    late_all,
    columns_g,
    wt,
    wn,
    wot,
    won,
    tile_a,
    tile_b,
    tile_g,
    field,
    zhat,
    zscale,
    xhat,
    xscale,
    value_l,
    sig_l,
    value_r,
    sig_r,
    gate,
    upd,
    du,
    part,
    dp,
    dz,
    send,
    recv,
    own,
    fetched,
):
    C, rows, J, groups, across, devices = dims
    per = 16
    chunks = rows // per
    wide = per * J
    row, chan = lax.axis_index("row"), lax.axis_index("chan")
    me = row * groups + chan
    tile_i, tile_j = chan // across, lax.rem(chan, across)

    def place(to):
        return (to // groups, lax.rem(to, groups))

    small = [
        pltpu.make_async_copy(src, dst, fetched.at[n])
        for n, (src, dst) in enumerate(
            (
                (chain_far, chain_v),
                (w_in_far, w_in),
                (w_out_far, w_out),
                (gain_in_far, gain_in),
                (gain_mid_far, gain_mid),
            )
        )
    ]
    for copy in small:
        copy.start()
    barrier = pltpu.get_barrier_semaphore()

    def greet(step, carry):
        other = lax.rem(me + step, devices)
        pl.semaphore_signal(barrier, inc=1, device_id=place(other), device_id_type=MESH)
        return carry

    lax.fori_loop(1, devices, greet, 0)
    pl.semaphore_wait(barrier, devices - 1)

    def scatter(at, src, dst):
        def step(k, carry):
            other = lax.rem(me + k, devices)
            pltpu.make_async_remote_copy(
                src_ref=src.at[other],
                dst_ref=dst.at[me],
                send_sem=send.at[at],
                recv_sem=recv.at[at],
                device_id=place(other),
                device_id_type=MESH,
            ).start()
            return carry

        lax.fori_loop(1, devices, step, 0)
        pltpu.make_async_copy(src.at[me], dst.at[me], own.at[at]).start()

    chips, core = devices // 2, lax.rem(me, 2)
    chip = me // 2

    def over_chips(at, source, dst):
        def step(k, carry):
            other = lax.rem(chip + k, chips)
            pltpu.make_async_remote_copy(
                src_ref=source(other),
                dst_ref=dst,
                send_sem=send.at[at],
                recv_sem=recv.at[at],
                device_id=place(2 * other + core),
                device_id_type=MESH,
            ).start()
            return carry

        lax.fori_loop(1, chips, step, 0)

    def to_sibling(at, src, dst):
        return pltpu.make_async_remote_copy(
            src_ref=src,
            dst_ref=dst,
            send_sem=send.at[at],
            recv_sem=recv.at[at],
            device_id=place(2 * chip + 1 - core),
            device_id_type=MESH,
        )

    def over_chan(at, source, dst):
        def step(k, carry):
            other = lax.rem(chan + 5 * k, groups)
            pltpu.make_async_remote_copy(
                src_ref=source(other),
                dst_ref=dst.at[chan],
                send_sem=send.at[at],
                recv_sem=recv.at[at],
                device_id=(row, other),
                device_id_type=MESH,
            ).start()
            return carry

        lax.fori_loop(1, groups, step, 0)
        pltpu.make_async_copy(source(chan), dst.at[chan], own.at[at]).start()

    def over_rows(at, src, dst):
        def step(k, carry):
            other = lax.rem(row + k, devices // groups)
            pltpu.make_async_remote_copy(
                src_ref=src,
                dst_ref=dst.at[row],
                send_sem=send.at[at],
                recv_sem=recv.at[at],
                device_id=(other, chan),
                device_id_type=MESH,
            ).start()
            return carry

        lax.fori_loop(1, devices // groups, step, 0)
        pltpu.make_async_copy(src, dst.at[row], own.at[at]).start()

    def landed_late(at, like):
        rest = like.at[pl.ds(0, like.shape[0] - 1)]
        return to_sibling(at, rest, rest)

    def arrive_late(at, like):
        pltpu.make_async_copy(like.at[0], like.at[0], own.at[at]).wait()
        landed_late(at, like).wait_recv()

    def landed_chips(at):
        rest = sums_in.at[pl.ds(0, chips - 1)]
        return to_sibling(at, rest, rest)

    def landed(at, like):
        rest = like.at[pl.ds(0, devices - 1)]
        return pltpu.make_async_remote_copy(
            src_ref=rest,
            dst_ref=rest,
            send_sem=send.at[at],
            recv_sem=recv.at[at],
            device_id=(row, chan),
            device_id_type=MESH,
        )

    def arrive(at, like):
        pltpu.make_async_copy(like.at[0], like.at[0], own.at[at]).wait()
        landed(at, like).wait_recv()

    own_c = C // groups
    every = (0, groups)
    quarters = [(q * groups // 4, (q + 1) * groups // 4) for q in range(4)]

    def tile_of(ref, other):
        first = pl.multiple_of((other // across) * rows, rows)
        left = pl.multiple_of(lax.rem(other, across) * J, J)
        return ref.at[:, pl.ds(first, rows), pl.ds(left, J)]

    def channels(ref, other):
        return ref.at[pl.ds(pl.multiple_of(other * own_c, own_c), own_c)]

    def to_cells(at, src, dst, piece):
        def step(k, carry):
            other = lax.rem(chan + 5 * k, groups)
            pltpu.make_async_remote_copy(
                src_ref=tile_of(src, other),
                dst_ref=channels(dst, chan),
                send_sem=send.at[at],
                recv_sem=recv.at[at],
                device_id=(row, other),
                device_id_type=MESH,
            ).start()
            return carry

        lax.fori_loop(max(1, piece[0]), piece[1], step, 0)
        if piece[0] == 0:
            pltpu.make_async_copy(tile_of(src, chan), channels(dst, chan), own.at[at]).start()

    def from_cells(at, src, dst, piece):
        def step(k, carry):
            other = lax.rem(chan + 5 * k, groups)
            pltpu.make_async_remote_copy(
                src_ref=channels(src, other),
                dst_ref=tile_of(dst, chan),
                send_sem=send.at[at],
                recv_sem=recv.at[at],
                device_id=(row, other),
                device_id_type=MESH,
            ).start()
            return carry

        lax.fori_loop(max(1, piece[0]), piece[1], step, 0)
        if piece[0] == 0:
            pltpu.make_async_copy(channels(src, chan), tile_of(dst, chan), own.at[at]).start()

    def landed_chan(at, like):
        rest = like.at[pl.ds(0, C - own_c)]
        return pltpu.make_async_remote_copy(
            src_ref=rest,
            dst_ref=rest,
            send_sem=send.at[at],
            recv_sem=recv.at[at],
            device_id=(row, chan),
            device_id_type=MESH,
        )

    def arrive_chan(at, like):
        part = like.at[pl.ds(0, own_c)]
        pltpu.make_async_copy(part, part, own.at[at]).wait()
        landed_chan(at, like).wait_recv()

    block = C // 8

    def unpack(box, tile):
        @pl.loop(0, 8)
        def _(n):
            some = box[pl.ds(n * block, block)].astype(f32)
            first = pl.multiple_of(n * block * rows, block * rows)
            tile[pl.ds(first, block * rows), :] = some.reshape(block * rows, J)

    def pack(tile, box):
        @pl.loop(0, 8)
        def _(n):
            first = pl.multiple_of(n * block * rows, block * rows)
            some = tile[pl.ds(first, block * rows), :]
            box[pl.ds(n * block, block)] = some.reshape(block, rows, J).astype(bf16)

    def load(tile, n):
        return jnp.concatenate(
            [tile[pl.ds(n * per + s, C, stride=rows), :] for s in range(per)], axis=1
        )

    def store(tile, n, value):
        for s in range(per):
            tile[pl.ds(n * per + s, C, stride=rows), :] = value[:, s * J : (s + 1) * J]

    def lanes(n):
        return pl.ds(pl.multiple_of(n * wide, wide), wide)

    first_row = row * (rows * groups // across) + tile_i * rows

    def mask(n):
        columns = (chain_v[pl.ds(tile_j, 1), :] > 0).astype(f32)
        return jnp.concatenate(
            [
                columns * (chain_s[first_row + n * per + s] > 0).astype(f32)
                for s in range(per)
            ],
            axis=1,
        )

    def matrix(box):
        high = devices // across
        tiles = box[...].reshape(high, across, rows, J)
        return jnp.concatenate(
            [tiles[:, t].reshape(high * rows, J) for t in range(across)], axis=1
        )

    def to_tiles(value, box):
        high = devices // across
        value = value.astype(bf16)
        for i in range(high):
            for t in range(across):
                box[i * across + t] = value[i * rows : (i + 1) * rows, t * J : (t + 1) * J]

    to_cells(PAIR, pair, cells_in.at[0], every)
    to_cells(GRAD, grad, cells_in.at[1], quarters[0])
    for copy in small:
        copy.wait()
    for u in range(2):
        turned = jnp.transpose(w_in[u].astype(f32)) * gain_in[pl.ds(u, 1), :]
        wt[u] = turned.astype(bf16)
        wn[u] = jnp.transpose(turned).astype(bf16)
        turned = jnp.transpose(w_out[u].astype(f32)) * gain_mid[pl.ds(u, 1), :]
        wot[u] = turned.astype(bf16)
        won[u] = jnp.transpose(turned).astype(bf16)
        for at, gain in ((u, gain_in), (2 + u, gain_mid)):
            scaled = gain[pl.ds(u, 1), :] * (1.0 / (J * across))
            columns_g[at] = jnp.transpose(jnp.broadcast_to(scaled, (C, C)))

    def side(u, n, at, value, sig, tile):
        p = nn(wt[u, 2 * at * C : 2 * (at + 1) * C, :], zhat[u, :, lanes(n)])
        v, s = p[:C], sigmoid(p[C:])
        value[u, :, lanes(n)] = v
        sig[u, :, lanes(n)] = s
        store(tile, n, mask(n) * s * v)

    def prepare(u, at_l, at_r):
        pack(tile_a, outbox.at[at_l])
        scatter(at_l, outbox.at[at_l], inbox.at[at_l])

        @pl.loop(0, chunks)
        def _(n):
            side(u, n, 1, value_r, sig_r, tile_b)

        pack(tile_b, outbox.at[at_r])
        scatter(at_r, outbox.at[at_r], inbox.at[at_r])

        @pl.loop(0, chunks)
        def _(n):
            p = nn(wt[u, 4 * C :, :], zhat[u, :, lanes(n)])
            gate[u, :, lanes(n)] = sigmoid(p).astype(bf16).astype(f32)

    arrive_chan(PAIR, cells_in.at[0])
    unpack(cells_in.at[0], tile_b)

    @pl.loop(0, chunks)
    def _(n):
        z = load(tile_b, n)
        field[0, :, lanes(n)] = z
        normed, scale = norm(z)
        zhat[0, :, lanes(n)] = normed.astype(bf16)
        zscale[0, :, lanes(n)] = scale
        side(0, n, 0, value_l, sig_l, tile_a)

    prepare(0, L0, R0)
    to_cells(GRAD, grad, cells_in.at[1], quarters[1])
    arrive(L0, inbox.at[L0])
    arrive(R0, inbox.at[R0])
    to_tiles(nt(matrix(inbox.at[L0]), matrix(inbox.at[R0])), outbox.at[X0])
    scatter(X0, outbox.at[X0], inbox.at[X0])
    to_cells(GRAD, grad, cells_in.at[1], quarters[2])

    arrive(X0, inbox.at[X0])
    unpack(inbox.at[X0], tile_b)

    @pl.loop(0, chunks)
    def _(n):
        normed, scale = norm(load(tile_b, n))
        normed = normed.astype(bf16)
        xhat[0, :, lanes(n)] = normed
        xscale[:, lanes(n)] = scale
        update = nn(wot[0], normed)
        upd[:, lanes(n)] = update
        z = (field[0, :, lanes(n)] + gate[0, :, lanes(n)] * update).astype(bf16).astype(f32)
        field[1, :, lanes(n)] = z
        normed, scale = norm(z)
        zhat[1, :, lanes(n)] = normed.astype(bf16)
        zscale[1, :, lanes(n)] = scale
        side(1, n, 0, value_l, sig_l, tile_a)

    prepare(1, L1, R1)
    to_cells(GRAD, grad, cells_in.at[1], quarters[3])
    arrive(L1, inbox.at[L1])
    arrive(R1, inbox.at[R1])
    to_tiles(tn(matrix(inbox.at[L1]), matrix(inbox.at[R1])), outbox.at[X1])
    scatter(X1, outbox.at[X1], inbox.at[X1])
    arrive_chan(GRAD, cells_in.at[1])
    unpack(cells_in.at[1], tile_g)

    def finish_back(u, n, cotangent):
        back = (cotangent * gate[u, :, lanes(n)]).astype(bf16)
        du[u, :, lanes(n)] = back
        return nn(won[u], back)

    @pl.loop(0, chunks)
    def _(n):
        part[:, lanes(n)] = finish_back(1, n, load(tile_g, n))

    arrive(X1, inbox.at[X1])
    unpack(inbox.at[X1], tile_b)

    @pl.loop(0, chunks)
    def _(n):
        normed, scale = norm(load(tile_b, n))
        xhat[1, :, lanes(n)] = normed.astype(bf16)
        store(tile_a, n, norm_back(part[:, lanes(n)], normed, scale))

    pack(tile_a, outbox.at[DX1])
    scatter(DX1, outbox.at[DX1], inbox.at[DX1])

    def gate_back(u, n, cotangent, update):
        s = gate[u, :, lanes(n)]
        back = (cotangent * update).astype(bf16).astype(f32)
        dp[4 * C :, lanes(n)] = (back * s * (1.0 - s)).astype(bf16)

    @pl.loop(0, chunks)
    def _(n):
        update = nn(wot[1], xhat[1, :, lanes(n)])
        store(tile_b, n, field[1, :, lanes(n)] + gate[1, :, lanes(n)] * update)
        gate_back(1, n, load(tile_g, n), update)

    pack(tile_b, cells_out.at[0])
    from_cells(POUT, cells_out.at[0], pair_out, quarters[0])

    arrive(DX1, inbox.at[DX1])
    to_tiles(nt(matrix(inbox.at[R1]), matrix(inbox.at[DX1])), outbox.at[DL1])
    scatter(DL1, outbox.at[DL1], inbox.at[DL1])
    to_tiles(nn(matrix(inbox.at[L1]), matrix(inbox.at[DX1])), outbox.at[DR1])
    scatter(DR1, outbox.at[DR1], inbox.at[DR1])
    from_cells(POUT, cells_out.at[0], pair_out, quarters[1])

    def side_back(u, n, at, value, sig, tile):
        s = sig[u, :, lanes(n)]
        back = load(tile, n) * mask(n) * s
        dp[2 * at * C : (2 * at + 1) * C, lanes(n)] = back.astype(bf16)
        back = back * value[u, :, lanes(n)] * (1.0 - s)
        dp[(2 * at + 1) * C : 2 * (at + 1) * C, lanes(n)] = back.astype(bf16)

    def left_back(u, at):
        arrive(at, inbox.at[at])
        unpack(inbox.at[at], tile_a)

        @pl.loop(0, chunks)
        def _(n):
            side_back(u, n, 0, value_l, sig_l, tile_a)
            part[:, lanes(n)] = nn(wn[u, :, : 2 * C], dp[: 2 * C, lanes(n)]) + nn(
                wn[u, :, 4 * C :], dp[4 * C :, lanes(n)]
            )

    def prepare_back(u, n):
        right = nn(wn[u, :, 2 * C : 4 * C], dp[2 * C : 4 * C, lanes(n)])
        return norm_back(
            part[:, lanes(n)] + right, zhat[u, :, lanes(n)].astype(f32), zscale[u, :, lanes(n)]
        )

    left_back(1, DL1)
    arrive(DR1, inbox.at[DR1])
    unpack(inbox.at[DR1], tile_b)

    @pl.loop(0, chunks)
    def _(n):
        side_back(1, n, 1, value_r, sig_r, tile_b)
        cotangent = (load(tile_g, n) + prepare_back(1, n)).astype(bf16).astype(f32)
        dz[:, lanes(n)] = cotangent
        back = finish_back(0, n, cotangent)
        store(tile_a, n, norm_back(back, xhat[0, :, lanes(n)].astype(f32), xscale[:, lanes(n)]))

    pack(tile_a, outbox.at[DX0])
    scatter(DX0, outbox.at[DX0], inbox.at[DX0])

    from_cells(POUT, cells_out.at[0], pair_out, quarters[2])

    def lay(at, value):
        for t in range(value.shape[1] // C):
            tile_s[pl.ds(at + t, C, stride=SUM_ROWS), :] = value[:, t * C : (t + 1) * C]

    lay(AT_IN1, nt(zhat[1], dp[...]))
    lay(AT_OUT[1], nt(xhat[1], du[1]))
    lay(AT_OUT[0], nt(xhat[0], du[0]))

    @pl.loop(0, chunks)
    def _(n):
        gate_back(0, n, dz[:, lanes(n)], upd[:, lanes(n)])

    lay(AT_GATE0, nt(zhat[0], dp[4 * C :]))
    half = chips // 8

    @pl.loop(0, 8)
    def _(n):
        first = pl.multiple_of(n * block * SUM_ROWS, block * SUM_ROWS)
        some = tile_s[pl.ds(first, block * SUM_ROWS), :]
        sums[pl.ds(n * half, half)] = some.reshape(half, 2, SUM_ROWS, C)

    to_sibling(CORES, sums.at[:, 1 - core], sums_core).start()
    to_sibling(CORES, sums.at[:, 1 - core], sums_core).wait_recv()

    @pl.loop(0, 8)
    def _(n):
        some = pl.ds(n * half, half)
        sums_chip[some] = sums[some, core] + sums_core[some]

    over_chips(SCATTER, lambda other: sums_chip.at[other], sums_in.at[chip])
    pltpu.make_async_copy(sums_chip.at[chip], sums_in.at[chip], own.at[SCATTER]).start()

    arrive(DX0, inbox.at[DX0])
    to_tiles(nn(matrix(inbox.at[DX0]), matrix(inbox.at[R0])), outbox.at[DL0])
    scatter(DL0, outbox.at[DL0], inbox.at[DL0])
    to_tiles(tn(matrix(inbox.at[DX0]), matrix(inbox.at[L0])), outbox.at[DR0])
    scatter(DR0, outbox.at[DR0], inbox.at[DR0])
    pltpu.make_async_copy(sums_chip.at[chip], sums_in.at[chip], own.at[SCATTER]).wait()
    landed_chips(SCATTER).wait_recv()
    total[...] = jnp.sum(sums_in[...], axis=0)
    over_chips(GATHER, lambda other: total, totals.at[core, chip])
    pltpu.make_async_copy(total, totals.at[core, chip], own.at[GATHER]).start()
    from_cells(POUT, cells_out.at[0], pair_out, quarters[3])

    left_back(0, DL0)

    def lay_late(at, value):
        for t in range(value.shape[1] // C):
            late[pl.ds(at + t, C, stride=LATE_ROWS), :] = value[:, t * C : (t + 1) * C]

    lay_late(0, nt(zhat[0], dp[: 2 * C]))
    arrive(DR0, inbox.at[DR0])
    unpack(inbox.at[DR0], tile_b)

    @pl.loop(0, chunks)
    def _(n):
        side_back(0, n, 1, value_r, sig_r, tile_b)

    lay_late(2, nt(zhat[0], dp[2 * C : 4 * C]))
    late_out[...] = late[...].reshape(late_out.shape).astype(bf16)
    over_chan(LATE_CHAN, lambda other: late_out.at[other], late_in)
    pltpu.make_async_copy(total, totals.at[core, chip], own.at[GATHER]).wait()
    landed_chips(GATHER).wait_recv()
    share = to_sibling(SHARE, totals.at[core], totals.at[core])
    share.start()

    @pl.loop(0, chunks)
    def _(n):
        store(tile_a, n, dz[:, lanes(n)] + prepare_back(0, n))

    pack(tile_a, cells_out.at[1])
    from_cells(GOUT, cells_out.at[1], grad_pair, (0, groups // 2))

    arrive_late(LATE_CHAN, late_in)
    late_part[...] = jnp.sum(late_in[...].astype(f32), axis=0).astype(bf16)
    over_rows(LATE_ROW, late_part, late_rows)
    from_cells(GOUT, cells_out.at[1], grad_pair, (groups // 2, groups))
    share.wait_recv()

    @pl.loop(0, 8)
    def _(n):
        some = pl.ds(n * half, half)
        both = jnp.stack([totals[0, some], totals[1, some]], axis=1)
        first = pl.multiple_of(n * block * SUM_ROWS, block * SUM_ROWS)
        tile_s[pl.ds(first, block * SUM_ROWS), :] = both.reshape(block * SUM_ROWS, C)

    def put(u, at, weights, d_weights, d_gain, fetch):
        both = jnp.zeros((C, C), f32)
        for t in range(weights.shape[2] // C):
            columns_t = slice(t * C, (t + 1) * C)
            rows_sum = fetch(t)
            d_weights[u, :, columns_t] = rows_sum * columns_g[at]
            both = both + rows_sum * weights[u, :, columns_t].astype(f32)
        row_sum = jnp.sum(jnp.transpose(both), axis=0, keepdims=True)
        d_gain[pl.ds(u, 1), :] = row_sum * (1.0 / (J * across))

    def early(at):
        return tile_s[pl.ds(at, C, stride=SUM_ROWS), :]

    def last(t):
        return late[pl.ds(t, C, stride=LATE_ROWS), :] if t < LATE_ROWS else early(AT_GATE0)

    arrive_late(LATE_ROW, late_rows)
    late_sum[...] = jnp.sum(late_rows[...].astype(f32), axis=0).astype(bf16)
    over_chan(LATE_ALL, lambda other: late_sum, late_all)
    put(1, 1, w_in, d_w_in, d_gain_in, lambda t: early(AT_IN1 + t))
    put(0, 2, w_out, d_w_out, d_gain_mid, lambda t: early(AT_OUT[0]))
    put(1, 3, w_out, d_w_out, d_gain_mid, lambda t: early(AT_OUT[1]))

    arrive_late(LATE_ALL, late_all)
    late[...] = late_all[...].astype(f32).reshape(late.shape)
    put(0, 0, w_in, d_w_in, d_gain_in, last)

    arrive_chan(POUT, cells_out.at[0])
    arrive_chan(GOUT, cells_out.at[1])
    for at in range(12):
        landed(at, outbox.at[at]).wait_send()
    for at in range(PAIR, GOUT + 1):
        landed_chan(at, cells_out.at[0]).wait_send()
    to_sibling(CORES, sums.at[:, 1 - core], sums_core).wait_send()
    landed_chips(SCATTER).wait_send()
    landed_chips(GATHER).wait_send()
    share.wait_send()
    landed_late(LATE_CHAN, late_in).wait_send()
    landed_late(LATE_ROW, late_rows).wait_send()
    landed_late(LATE_ALL, late_all).wait_send()


def hand_on(*refs):
    count = len(refs) // 2
    for got, out in zip(refs[:count], refs[count:]):
        out[...] = got[...]


def local(groups, pair, grad_out, residue_chain, gain_in, w_in, gain_mid, w_out):
    C = w_in.shape[1]
    own_c, own_rows, size = pair.shape
    devices = C
    across = 4 if groups == 16 else 2
    J = size // across
    rows = own_rows * across // groups
    cells = rows * J
    dims = (C, rows, J, groups, across, devices)
    whole = pl.BlockSpec(memory_space=pltpu.VMEM)
    far = pl.BlockSpec(memory_space=pl.ANY)
    box = (C, rows, J)
    late_rows = C // groups * LATE_ROWS
    got = pl.pallas_call(
        partial(kernel, dims),
        out_shape=[
            jax.ShapeDtypeStruct(pair.shape, bf16),
            jax.ShapeDtypeStruct(pair.shape, bf16),
            jax.ShapeDtypeStruct(gain_in.shape, f32),
            jax.ShapeDtypeStruct(w_in.shape, f32),
            jax.ShapeDtypeStruct(gain_mid.shape, f32),
            jax.ShapeDtypeStruct(w_out.shape, f32),
        ],
        in_specs=[far, far, pl.BlockSpec(memory_space=pltpu.SMEM)] + [far] * 5,
        out_specs=[whole] * 6,
        scratch_shapes=[
            pltpu.VMEM((across, J), jnp.int32),
            pltpu.VMEM(w_in.shape, bf16),
            pltpu.VMEM(w_out.shape, bf16),
            pltpu.VMEM(gain_in.shape, f32),
            pltpu.VMEM(gain_mid.shape, f32),
            pltpu.VMEM((12,) + box, bf16),
            pltpu.VMEM((12,) + box, bf16),
            pltpu.VMEM((2,) + box, bf16),
            pltpu.VMEM((2,) + box, bf16),
            pltpu.VMEM((C // 2, 2, SUM_ROWS, C), f32),
            pltpu.VMEM((C // 2, SUM_ROWS, C), f32),
            pltpu.VMEM((C // 2, SUM_ROWS, C), f32),
            pltpu.VMEM((C // 2, SUM_ROWS, C), f32),
            pltpu.VMEM((SUM_ROWS, C), f32),
            pltpu.VMEM((2, C // 2, SUM_ROWS, C), f32),
            pltpu.VMEM((C * SUM_ROWS, C), f32),
            pltpu.VMEM((C * LATE_ROWS, C), f32),
            pltpu.VMEM((groups, late_rows, C), bf16),
            pltpu.VMEM((groups, late_rows, C), bf16),
            pltpu.VMEM((late_rows, C), bf16),
            pltpu.VMEM((devices // groups, late_rows, C), bf16),
            pltpu.VMEM((late_rows, C), bf16),
            pltpu.VMEM((groups, late_rows, C), bf16),
            pltpu.VMEM((4, C, C), f32),
            pltpu.VMEM((2, 5 * C, C), bf16),
            pltpu.VMEM((2, C, 5 * C), bf16),
            pltpu.VMEM((2, C, C), bf16),
            pltpu.VMEM((2, C, C), bf16),
            pltpu.VMEM((C * rows, J), f32),
            pltpu.VMEM((C * rows, J), f32),
            pltpu.VMEM((C * rows, J), f32),
            pltpu.VMEM((2, C, cells), f32),
            pltpu.VMEM((2, C, cells), bf16),
            pltpu.VMEM((2, 1, cells), f32),
            pltpu.VMEM((2, C, cells), bf16),
            pltpu.VMEM((1, cells), f32),
            pltpu.VMEM((2, C, cells), f32),
            pltpu.VMEM((2, C, cells), f32),
            pltpu.VMEM((2, C, cells), f32),
            pltpu.VMEM((2, C, cells), f32),
            pltpu.VMEM((2, C, cells), f32),
            pltpu.VMEM((C, cells), f32),
            pltpu.VMEM((2, C, cells), bf16),
            pltpu.VMEM((C, cells), f32),
            pltpu.VMEM((5 * C, cells), bf16),
            pltpu.VMEM((C, cells), f32),
            pltpu.SemaphoreType.DMA((EXCHANGES,)),
            pltpu.SemaphoreType.DMA((EXCHANGES,)),
            pltpu.SemaphoreType.DMA((EXCHANGES,)),
            pltpu.SemaphoreType.DMA((5,)),
        ],
        compiler_params=pltpu.CompilerParams(
            collective_id=0, has_side_effects=True, vmem_limit_bytes=60 * 2**20
        ),
    )(
        pair,
        grad_out,
        residue_chain,
        residue_chain.reshape(across, J),
        w_in,
        w_out,
        gain_in,
        gain_mid,
    )
    return pl.pallas_call(
        hand_on,
        out_shape=[jax.ShapeDtypeStruct(g.shape, g.dtype) for g in got],
        in_specs=[whole] * len(got),
        out_specs=[whole] * len(got),
    )(*got)


def solution(mesh):
    return jax.shard_map(
        partial(local, mesh.shape["chan"]),
        mesh=mesh,
        in_specs=(P("chan", "row", None), P("chan", "row", None), P(), P(), P(), P(), P()),
        out_specs=(P("chan", "row", None), P("chan", "row", None), P(), P(), P(), P()),
        check_vma=False,
    )
```

```python
from functools import partial

import jax
import jax.numpy as jnp
from jax import lax
from jax.experimental import pallas as pl
from jax.experimental.pallas import tpu as pltpu
from jax.sharding import PartitionSpec as P

epsilon = 1e-05
MESH = pl.DeviceIdType.MESH
f32 = jnp.float32
bf16 = jnp.bfloat16

L0, R0, X0, L1, R1, X1, DX1, DL1, DR1, DX0, DL0, DR0 = range(12)
PAIR, GRAD, POUT, GOUT = range(12, 16)
CORES, SCATTER, GATHER, SHARE = range(16, 20)
LATE_CHAN, LATE_ROW, LATE_ALL = range(20, 23)
EXCHANGES = 23
AT_IN1, AT_OUT, AT_GATE0 = 0, (6, 5), 7
SUM_ROWS = 8
LATE_ROWS = 4


def nn(a, b):
    return lax.dot_general(a, b, (((1,), (0,)), ((), ())), preferred_element_type=f32)


def nt(a, b):
    return lax.dot_general(a, b, (((1,), (1,)), ((), ())), preferred_element_type=f32)


def tn(a, b):
    return lax.dot_general(a, b, (((0,), (0,)), ((), ())), preferred_element_type=f32)


def sigmoid(x):
    return 0.5 * jnp.tanh(0.5 * x) + 0.5


def norm(z):
    center = z - jnp.mean(z, axis=0, keepdims=True)
    scale = lax.rsqrt(jnp.mean(center * center, axis=0, keepdims=True) + epsilon)
    return center * scale, scale


def norm_back(grad, normed, scale):
    mean_grad = jnp.mean(grad, axis=0, keepdims=True)
    mean_both = jnp.mean(grad * normed, axis=0, keepdims=True)
    return scale * (grad - mean_grad - normed * mean_both)


def kernel(
    dims,
    pair,
    grad,
    chain_s,
    chain_far,
    w_in_far,
    w_out_far,
    gain_in_far,
    gain_mid_far,
    pair_out,
    grad_pair,
    d_gain_in,
    d_w_in,
    d_gain_mid,
    d_w_out,
    chain_v,
    w_in,
    w_out,
    gain_in,
    gain_mid,
    outbox,
    inbox,
    cells_out,
    cells_in,
    sums,
    sums_core,
    sums_chip,
    sums_in,
    total,
    totals,
    tile_s,
    late,
    late_out,
    late_in,
    late_part,
    late_rows,
    late_sum,
    late_all,
    columns_g,
    wt,
    wn,
    wot,
    won,
    tile_a,
    tile_b,
    tile_g,
    field,
    zhat,
    zscale,
    xhat,
    xscale,
    value_l,
    sig_l,
    value_r,
    sig_r,
    gate,
    upd,
    du,
    part,
    dp,
    dz,
    send,
    recv,
    own,
    fetched,
):
    C, rows, J, groups, across, devices = dims
    per = 16
    chunks = rows // per
    wide = per * J
    row, chan = lax.axis_index("row"), lax.axis_index("chan")
    me = row * groups + chan
    tile_i, tile_j = chan // across, lax.rem(chan, across)

    def place(to):
        return (to // groups, lax.rem(to, groups))

    small = [
        pltpu.make_async_copy(src, dst, fetched.at[n])
        for n, (src, dst) in enumerate(
            (
                (chain_far, chain_v),
                (w_in_far, w_in),
                (w_out_far, w_out),
                (gain_in_far, gain_in),
                (gain_mid_far, gain_mid),
            )
        )
    ]
    for copy in small:
        copy.start()
    barrier = pltpu.get_barrier_semaphore()

    def greet(step, carry):
        other = lax.rem(me + step, devices)
        pl.semaphore_signal(barrier, inc=1, device_id=place(other), device_id_type=MESH)
        return carry

    lax.fori_loop(1, devices, greet, 0)
    pl.semaphore_wait(barrier, devices - 1)

    def scatter(at, src, dst):
        def step(k, carry):
            other = lax.rem(me + k, devices)
            pltpu.make_async_remote_copy(
                src_ref=src.at[other],
                dst_ref=dst.at[me],
                send_sem=send.at[at],
                recv_sem=recv.at[at],
                device_id=place(other),
                device_id_type=MESH,
            ).start()
            return carry

        lax.fori_loop(1, devices, step, 0)
        pltpu.make_async_copy(src.at[me], dst.at[me], own.at[at]).start()

    chips, core = devices // 2, lax.rem(me, 2)
    chip = me // 2

    def over_chips(at, source, dst):
        def step(k, carry):
            other = lax.rem(chip + k, chips)
            pltpu.make_async_remote_copy(
                src_ref=source(other),
                dst_ref=dst,
                send_sem=send.at[at],
                recv_sem=recv.at[at],
                device_id=place(2 * other + core),
                device_id_type=MESH,
            ).start()
            return carry

        lax.fori_loop(1, chips, step, 0)

    def to_sibling(at, src, dst):
        return pltpu.make_async_remote_copy(
            src_ref=src,
            dst_ref=dst,
            send_sem=send.at[at],
            recv_sem=recv.at[at],
            device_id=place(2 * chip + 1 - core),
            device_id_type=MESH,
        )

    def over_chan(at, source, dst):
        def step(k, carry):
            other = lax.rem(chan + 5 * k, groups)
            pltpu.make_async_remote_copy(
                src_ref=source(other),
                dst_ref=dst.at[chan],
                send_sem=send.at[at],
                recv_sem=recv.at[at],
                device_id=(row, other),
                device_id_type=MESH,
            ).start()
            return carry

        lax.fori_loop(1, groups, step, 0)
        pltpu.make_async_copy(source(chan), dst.at[chan], own.at[at]).start()

    def over_rows(at, src, dst):
        def step(k, carry):
            other = lax.rem(row + k, devices // groups)
            pltpu.make_async_remote_copy(
                src_ref=src,
                dst_ref=dst.at[row],
                send_sem=send.at[at],
                recv_sem=recv.at[at],
                device_id=(other, chan),
                device_id_type=MESH,
            ).start()
            return carry

        lax.fori_loop(1, devices // groups, step, 0)
        pltpu.make_async_copy(src, dst.at[row], own.at[at]).start()

    def landed_late(at, like):
        rest = like.at[pl.ds(0, like.shape[0] - 1)]
        return to_sibling(at, rest, rest)

    def arrive_late(at, like):
        pltpu.make_async_copy(like.at[0], like.at[0], own.at[at]).wait()
        landed_late(at, like).wait_recv()

    def landed_chips(at):
        rest = sums_in.at[pl.ds(0, chips - 1)]
        return to_sibling(at, rest, rest)

    def landed(at, like):
        rest = like.at[pl.ds(0, devices - 1)]
        return pltpu.make_async_remote_copy(
            src_ref=rest,
            dst_ref=rest,
            send_sem=send.at[at],
            recv_sem=recv.at[at],
            device_id=(row, chan),
            device_id_type=MESH,
        )

    def arrive(at, like):
        pltpu.make_async_copy(like.at[0], like.at[0], own.at[at]).wait()
        landed(at, like).wait_recv()

    own_c = C // groups
    every = (0, groups)
    quarters = [(q * groups // 4, (q + 1) * groups // 4) for q in range(4)]

    def tile_of(ref, other):
        first = pl.multiple_of((other // across) * rows, rows)
        left = pl.multiple_of(lax.rem(other, across) * J, J)
        return ref.at[:, pl.ds(first, rows), pl.ds(left, J)]

    def channels(ref, other):
        return ref.at[pl.ds(pl.multiple_of(other * own_c, own_c), own_c)]

    def to_cells(at, src, dst, piece):
        def step(k, carry):
            other = lax.rem(chan + 5 * k, groups)
            pltpu.make_async_remote_copy(
                src_ref=tile_of(src, other),
                dst_ref=channels(dst, chan),
                send_sem=send.at[at],
                recv_sem=recv.at[at],
                device_id=(row, other),
                device_id_type=MESH,
            ).start()
            return carry

        lax.fori_loop(max(1, piece[0]), piece[1], step, 0)
        if piece[0] == 0:
            pltpu.make_async_copy(tile_of(src, chan), channels(dst, chan), own.at[at]).start()

    def from_cells(at, src, dst, piece):
        def step(k, carry):
            other = lax.rem(chan + 5 * k, groups)
            pltpu.make_async_remote_copy(
                src_ref=channels(src, other),
                dst_ref=tile_of(dst, chan),
                send_sem=send.at[at],
                recv_sem=recv.at[at],
                device_id=(row, other),
                device_id_type=MESH,
            ).start()
            return carry

        lax.fori_loop(max(1, piece[0]), piece[1], step, 0)
        if piece[0] == 0:
            pltpu.make_async_copy(channels(src, chan), tile_of(dst, chan), own.at[at]).start()

    def landed_chan(at, like):
        rest = like.at[pl.ds(0, C - own_c)]
        return pltpu.make_async_remote_copy(
            src_ref=rest,
            dst_ref=rest,
            send_sem=send.at[at],
            recv_sem=recv.at[at],
            device_id=(row, chan),
            device_id_type=MESH,
        )

    def arrive_chan(at, like):
        part = like.at[pl.ds(0, own_c)]
        pltpu.make_async_copy(part, part, own.at[at]).wait()
        landed_chan(at, like).wait_recv()

    block = C // 8

    def unpack(box, tile):
        @pl.loop(0, 8, unroll=4)
        def _(n):
            some = box[pl.ds(n * block, block)].astype(f32)
            first = pl.multiple_of(n * block * rows, block * rows)
            tile[pl.ds(first, block * rows), :] = some.reshape(block * rows, J)

    def pack(tile, box):
        @pl.loop(0, 8, unroll=4)
        def _(n):
            first = pl.multiple_of(n * block * rows, block * rows)
            some = tile[pl.ds(first, block * rows), :]
            box[pl.ds(n * block, block)] = some.reshape(block, rows, J).astype(bf16)

    def load(tile, n):
        return jnp.concatenate(
            [tile[pl.ds(n * per + s, C, stride=rows), :] for s in range(per)], axis=1
        )

    def store(tile, n, value):
        for s in range(per):
            tile[pl.ds(n * per + s, C, stride=rows), :] = value[:, s * J : (s + 1) * J]

    def lanes(n):
        return pl.ds(pl.multiple_of(n * wide, wide), wide)

    first_row = row * (rows * groups // across) + tile_i * rows

    def mask(n):
        columns = (chain_v[pl.ds(tile_j, 1), :] > 0).astype(f32)
        return jnp.concatenate(
            [
                columns * (chain_s[first_row + n * per + s] > 0).astype(f32)
                for s in range(per)
            ],
            axis=1,
        )

    def matrix(box):
        high = devices // across
        tiles = box[...].reshape(high, across, rows, J)
        return jnp.concatenate(
            [tiles[:, t].reshape(high * rows, J) for t in range(across)], axis=1
        )

    def to_tiles(value, box):
        high = devices // across
        value = value.astype(bf16)
        for i in range(high):
            for t in range(across):
                box[i * across + t] = value[i * rows : (i + 1) * rows, t * J : (t + 1) * J]

    to_cells(PAIR, pair, cells_in.at[0], every)
    to_cells(GRAD, grad, cells_in.at[1], quarters[0])
    for copy in small:
        copy.wait()
    for u in range(2):
        turned = jnp.transpose(w_in[u].astype(f32)) * gain_in[pl.ds(u, 1), :]
        wt[u] = turned.astype(bf16)
        wn[u] = jnp.transpose(turned).astype(bf16)
        turned = jnp.transpose(w_out[u].astype(f32)) * gain_mid[pl.ds(u, 1), :]
        wot[u] = turned.astype(bf16)
        won[u] = jnp.transpose(turned).astype(bf16)
        for at, gain in ((u, gain_in), (2 + u, gain_mid)):
            scaled = gain[pl.ds(u, 1), :] * (1.0 / (J * across))
            columns_g[at] = jnp.transpose(jnp.broadcast_to(scaled, (C, C)))

    def side(u, n, at, value, sig, tile):
        p = nn(wt[u, 2 * at * C : 2 * (at + 1) * C, :], zhat[u, :, lanes(n)])
        v, s = p[:C], sigmoid(p[C:])
        value[u, :, lanes(n)] = v
        sig[u, :, lanes(n)] = s
        store(tile, n, mask(n) * s * v)

    def prepare(u, at_l, at_r):
        pack(tile_a, outbox.at[at_l])
        scatter(at_l, outbox.at[at_l], inbox.at[at_l])

        @pl.loop(0, chunks)
        def _(n):
            side(u, n, 1, value_r, sig_r, tile_b)

        pack(tile_b, outbox.at[at_r])
        scatter(at_r, outbox.at[at_r], inbox.at[at_r])

        @pl.loop(0, chunks)
        def _(n):
            p = nn(wt[u, 4 * C :, :], zhat[u, :, lanes(n)])
            gate[u, :, lanes(n)] = sigmoid(p).astype(bf16).astype(f32)

    arrive_chan(PAIR, cells_in.at[0])
    unpack(cells_in.at[0], tile_b)

    @pl.loop(0, chunks)
    def _(n):
        z = load(tile_b, n)
        field[0, :, lanes(n)] = z
        normed, scale = norm(z)
        zhat[0, :, lanes(n)] = normed.astype(bf16)
        zscale[0, :, lanes(n)] = scale
        side(0, n, 0, value_l, sig_l, tile_a)

    prepare(0, L0, R0)
    to_cells(GRAD, grad, cells_in.at[1], quarters[1])
    arrive(L0, inbox.at[L0])
    arrive(R0, inbox.at[R0])
    to_tiles(nt(matrix(inbox.at[L0]), matrix(inbox.at[R0])), outbox.at[X0])
    scatter(X0, outbox.at[X0], inbox.at[X0])
    to_cells(GRAD, grad, cells_in.at[1], quarters[2])

    arrive(X0, inbox.at[X0])
    unpack(inbox.at[X0], tile_b)

    @pl.loop(0, chunks)
    def _(n):
        normed, scale = norm(load(tile_b, n))
        normed = normed.astype(bf16)
        xhat[0, :, lanes(n)] = normed
        xscale[:, lanes(n)] = scale
        update = nn(wot[0], normed)
        upd[:, lanes(n)] = update
        z = (field[0, :, lanes(n)] + gate[0, :, lanes(n)] * update).astype(bf16).astype(f32)
        field[1, :, lanes(n)] = z
        normed, scale = norm(z)
        zhat[1, :, lanes(n)] = normed.astype(bf16)
        zscale[1, :, lanes(n)] = scale
        side(1, n, 0, value_l, sig_l, tile_a)

    prepare(1, L1, R1)
    to_cells(GRAD, grad, cells_in.at[1], quarters[3])
    arrive(L1, inbox.at[L1])
    arrive(R1, inbox.at[R1])
    to_tiles(tn(matrix(inbox.at[L1]), matrix(inbox.at[R1])), outbox.at[X1])
    scatter(X1, outbox.at[X1], inbox.at[X1])
    arrive_chan(GRAD, cells_in.at[1])
    unpack(cells_in.at[1], tile_g)

    def finish_back(u, n, cotangent):
        back = (cotangent * gate[u, :, lanes(n)]).astype(bf16)
        du[u, :, lanes(n)] = back
        return nn(won[u], back)

    @pl.loop(0, chunks)
    def _(n):
        part[:, lanes(n)] = finish_back(1, n, load(tile_g, n))

    arrive(X1, inbox.at[X1])
    unpack(inbox.at[X1], tile_b)

    @pl.loop(0, chunks)
    def _(n):
        normed, scale = norm(load(tile_b, n))
        xhat[1, :, lanes(n)] = normed.astype(bf16)
        store(tile_a, n, norm_back(part[:, lanes(n)], normed, scale))

    pack(tile_a, outbox.at[DX1])
    scatter(DX1, outbox.at[DX1], inbox.at[DX1])

    def gate_back(u, n, cotangent, update):
        s = gate[u, :, lanes(n)]
        back = (cotangent * update).astype(bf16).astype(f32)
        dp[4 * C :, lanes(n)] = (back * s * (1.0 - s)).astype(bf16)

    @pl.loop(0, chunks)
    def _(n):
        update = nn(wot[1], xhat[1, :, lanes(n)])
        store(tile_b, n, field[1, :, lanes(n)] + gate[1, :, lanes(n)] * update)
        gate_back(1, n, load(tile_g, n), update)

    pack(tile_b, cells_out.at[0])
    from_cells(POUT, cells_out.at[0], pair_out, quarters[0])

    arrive(DX1, inbox.at[DX1])
    to_tiles(nt(matrix(inbox.at[R1]), matrix(inbox.at[DX1])), outbox.at[DL1])
    scatter(DL1, outbox.at[DL1], inbox.at[DL1])
    to_tiles(nn(matrix(inbox.at[L1]), matrix(inbox.at[DX1])), outbox.at[DR1])
    scatter(DR1, outbox.at[DR1], inbox.at[DR1])
    from_cells(POUT, cells_out.at[0], pair_out, quarters[1])

    def side_back(u, n, at, value, sig, tile):
        s = sig[u, :, lanes(n)]
        back = load(tile, n) * mask(n) * s
        dp[2 * at * C : (2 * at + 1) * C, lanes(n)] = back.astype(bf16)
        back = back * value[u, :, lanes(n)] * (1.0 - s)
        dp[(2 * at + 1) * C : 2 * (at + 1) * C, lanes(n)] = back.astype(bf16)

    def left_back(u, at):
        arrive(at, inbox.at[at])
        unpack(inbox.at[at], tile_a)

        @pl.loop(0, chunks)
        def _(n):
            side_back(u, n, 0, value_l, sig_l, tile_a)
            part[:, lanes(n)] = nn(wn[u, :, : 2 * C], dp[: 2 * C, lanes(n)]) + nn(
                wn[u, :, 4 * C :], dp[4 * C :, lanes(n)]
            )

    def prepare_back(u, n):
        right = nn(wn[u, :, 2 * C : 4 * C], dp[2 * C : 4 * C, lanes(n)])
        return norm_back(
            part[:, lanes(n)] + right, zhat[u, :, lanes(n)].astype(f32), zscale[u, :, lanes(n)]
        )

    left_back(1, DL1)
    arrive(DR1, inbox.at[DR1])
    unpack(inbox.at[DR1], tile_b)

    @pl.loop(0, chunks)
    def _(n):
        side_back(1, n, 1, value_r, sig_r, tile_b)
        cotangent = (load(tile_g, n) + prepare_back(1, n)).astype(bf16).astype(f32)
        dz[:, lanes(n)] = cotangent
        back = finish_back(0, n, cotangent)
        store(tile_a, n, norm_back(back, xhat[0, :, lanes(n)].astype(f32), xscale[:, lanes(n)]))

    pack(tile_a, outbox.at[DX0])
    scatter(DX0, outbox.at[DX0], inbox.at[DX0])

    from_cells(POUT, cells_out.at[0], pair_out, quarters[2])

    def lay(at, value):
        for t in range(value.shape[1] // C):
            tile_s[pl.ds(at + t, C, stride=SUM_ROWS), :] = value[:, t * C : (t + 1) * C]

    lay(AT_IN1, nt(zhat[1], dp[...]))
    lay(AT_OUT[1], nt(xhat[1], du[1]))
    lay(AT_OUT[0], nt(xhat[0], du[0]))

    @pl.loop(0, chunks)
    def _(n):
        gate_back(0, n, dz[:, lanes(n)], upd[:, lanes(n)])

    lay(AT_GATE0, nt(zhat[0], dp[4 * C :]))
    half = chips // 8

    @pl.loop(0, 8, unroll=4)
    def _(n):
        first = pl.multiple_of(n * block * SUM_ROWS, block * SUM_ROWS)
        some = tile_s[pl.ds(first, block * SUM_ROWS), :]
        sums[pl.ds(n * half, half)] = some.reshape(half, 2, SUM_ROWS, C)

    to_sibling(CORES, sums.at[:, 1 - core], sums_core).start()
    to_sibling(CORES, sums.at[:, 1 - core], sums_core).wait_recv()

    @pl.loop(0, 8, unroll=4)
    def _(n):
        some = pl.ds(n * half, half)
        sums_chip[some] = sums[some, core] + sums_core[some]

    over_chips(SCATTER, lambda other: sums_chip.at[other], sums_in.at[chip])
    pltpu.make_async_copy(sums_chip.at[chip], sums_in.at[chip], own.at[SCATTER]).start()

    arrive(DX0, inbox.at[DX0])
    to_tiles(nn(matrix(inbox.at[DX0]), matrix(inbox.at[R0])), outbox.at[DL0])
    scatter(DL0, outbox.at[DL0], inbox.at[DL0])
    to_tiles(tn(matrix(inbox.at[DX0]), matrix(inbox.at[L0])), outbox.at[DR0])
    scatter(DR0, outbox.at[DR0], inbox.at[DR0])
    pltpu.make_async_copy(sums_chip.at[chip], sums_in.at[chip], own.at[SCATTER]).wait()
    landed_chips(SCATTER).wait_recv()
    total[...] = jnp.sum(sums_in[...], axis=0)
    over_chips(GATHER, lambda other: total, totals.at[core, chip])
    pltpu.make_async_copy(total, totals.at[core, chip], own.at[GATHER]).start()
    from_cells(POUT, cells_out.at[0], pair_out, quarters[3])

    left_back(0, DL0)

    def lay_late(at, value):
        for t in range(value.shape[1] // C):
            late[pl.ds(at + t, C, stride=LATE_ROWS), :] = value[:, t * C : (t + 1) * C]

    lay_late(0, nt(zhat[0], dp[: 2 * C]))
    arrive(DR0, inbox.at[DR0])
    unpack(inbox.at[DR0], tile_b)

    @pl.loop(0, chunks)
    def _(n):
        side_back(0, n, 1, value_r, sig_r, tile_b)

    lay_late(2, nt(zhat[0], dp[2 * C : 4 * C]))
    late_out[...] = late[...].reshape(late_out.shape).astype(bf16)
    over_chan(LATE_CHAN, lambda other: late_out.at[other], late_in)
    pltpu.make_async_copy(total, totals.at[core, chip], own.at[GATHER]).wait()
    landed_chips(GATHER).wait_recv()
    share = to_sibling(SHARE, totals.at[core], totals.at[core])
    share.start()

    @pl.loop(0, chunks)
    def _(n):
        store(tile_a, n, dz[:, lanes(n)] + prepare_back(0, n))

    pack(tile_a, cells_out.at[1])
    from_cells(GOUT, cells_out.at[1], grad_pair, (0, groups // 2))

    arrive_late(LATE_CHAN, late_in)
    late_part[...] = jnp.sum(late_in[...].astype(f32), axis=0).astype(bf16)
    over_rows(LATE_ROW, late_part, late_rows)
    from_cells(GOUT, cells_out.at[1], grad_pair, (groups // 2, groups))
    share.wait_recv()

    @pl.loop(0, 8, unroll=4)
    def _(n):
        some = pl.ds(n * half, half)
        both = jnp.stack([totals[0, some], totals[1, some]], axis=1)
        first = pl.multiple_of(n * block * SUM_ROWS, block * SUM_ROWS)
        tile_s[pl.ds(first, block * SUM_ROWS), :] = both.reshape(block * SUM_ROWS, C)

    def put(u, at, weights, d_weights, d_gain, fetch):
        both = jnp.zeros((C, C), f32)
        for t in range(weights.shape[2] // C):
            columns_t = slice(t * C, (t + 1) * C)
            rows_sum = fetch(t)
            d_weights[u, :, columns_t] = rows_sum * columns_g[at]
            both = both + rows_sum * weights[u, :, columns_t].astype(f32)
        row_sum = jnp.sum(jnp.transpose(both), axis=0, keepdims=True)
        d_gain[pl.ds(u, 1), :] = row_sum * (1.0 / (J * across))

    def early(at):
        return tile_s[pl.ds(at, C, stride=SUM_ROWS), :]

    def last(t):
        return late[pl.ds(t, C, stride=LATE_ROWS), :] if t < LATE_ROWS else early(AT_GATE0)

    arrive_late(LATE_ROW, late_rows)
    late_sum[...] = jnp.sum(late_rows[...].astype(f32), axis=0).astype(bf16)
    over_chan(LATE_ALL, lambda other: late_sum, late_all)
    put(1, 1, w_in, d_w_in, d_gain_in, lambda t: early(AT_IN1 + t))
    put(0, 2, w_out, d_w_out, d_gain_mid, lambda t: early(AT_OUT[0]))
    put(1, 3, w_out, d_w_out, d_gain_mid, lambda t: early(AT_OUT[1]))

    arrive_late(LATE_ALL, late_all)
    late[...] = late_all[...].astype(f32).reshape(late.shape)
    put(0, 0, w_in, d_w_in, d_gain_in, last)

    arrive_chan(POUT, cells_out.at[0])
    arrive_chan(GOUT, cells_out.at[1])
    for at in range(12):
        landed(at, outbox.at[at]).wait_send()
    for at in range(PAIR, GOUT + 1):
        landed_chan(at, cells_out.at[0]).wait_send()
    to_sibling(CORES, sums.at[:, 1 - core], sums_core).wait_send()
    landed_chips(SCATTER).wait_send()
    landed_chips(GATHER).wait_send()
    share.wait_send()
    landed_late(LATE_CHAN, late_in).wait_send()
    landed_late(LATE_ROW, late_rows).wait_send()
    landed_late(LATE_ALL, late_all).wait_send()


def hand_on(*refs):
    count = len(refs) // 2
    for got, out in zip(refs[:count], refs[count:]):
        out[...] = got[...]


def local(groups, pair, grad_out, residue_chain, gain_in, w_in, gain_mid, w_out):
    C = w_in.shape[1]
    own_c, own_rows, size = pair.shape
    devices = C
    across = 4 if groups == 16 else 2
    J = size // across
    rows = own_rows * across // groups
    cells = rows * J
    dims = (C, rows, J, groups, across, devices)
    whole = pl.BlockSpec(memory_space=pltpu.VMEM)
    far = pl.BlockSpec(memory_space=pl.ANY)
    box = (C, rows, J)
    late_rows = C // groups * LATE_ROWS
    got = pl.pallas_call(
        partial(kernel, dims),
        out_shape=[
            jax.ShapeDtypeStruct(pair.shape, bf16),
            jax.ShapeDtypeStruct(pair.shape, bf16),
            jax.ShapeDtypeStruct(gain_in.shape, f32),
            jax.ShapeDtypeStruct(w_in.shape, f32),
            jax.ShapeDtypeStruct(gain_mid.shape, f32),
            jax.ShapeDtypeStruct(w_out.shape, f32),
        ],
        in_specs=[far, far, pl.BlockSpec(memory_space=pltpu.SMEM)] + [far] * 5,
        out_specs=[whole] * 6,
        scratch_shapes=[
            pltpu.VMEM((across, J), jnp.int32),
            pltpu.VMEM(w_in.shape, bf16),
            pltpu.VMEM(w_out.shape, bf16),
            pltpu.VMEM(gain_in.shape, f32),
            pltpu.VMEM(gain_mid.shape, f32),
            pltpu.VMEM((12,) + box, bf16),
            pltpu.VMEM((12,) + box, bf16),
            pltpu.VMEM((2,) + box, bf16),
            pltpu.VMEM((2,) + box, bf16),
            pltpu.VMEM((C // 2, 2, SUM_ROWS, C), f32),
            pltpu.VMEM((C // 2, SUM_ROWS, C), f32),
            pltpu.VMEM((C // 2, SUM_ROWS, C), f32),
            pltpu.VMEM((C // 2, SUM_ROWS, C), f32),
            pltpu.VMEM((SUM_ROWS, C), f32),
            pltpu.VMEM((2, C // 2, SUM_ROWS, C), f32),
            pltpu.VMEM((C * SUM_ROWS, C), f32),
            pltpu.VMEM((C * LATE_ROWS, C), f32),
            pltpu.VMEM((groups, late_rows, C), bf16),
            pltpu.VMEM((groups, late_rows, C), bf16),
            pltpu.VMEM((late_rows, C), bf16),
            pltpu.VMEM((devices // groups, late_rows, C), bf16),
            pltpu.VMEM((late_rows, C), bf16),
            pltpu.VMEM((groups, late_rows, C), bf16),
            pltpu.VMEM((4, C, C), f32),
            pltpu.VMEM((2, 5 * C, C), bf16),
            pltpu.VMEM((2, C, 5 * C), bf16),
            pltpu.VMEM((2, C, C), bf16),
            pltpu.VMEM((2, C, C), bf16),
            pltpu.VMEM((C * rows, J), f32),
            pltpu.VMEM((C * rows, J), f32),
            pltpu.VMEM((C * rows, J), f32),
            pltpu.VMEM((2, C, cells), f32),
            pltpu.VMEM((2, C, cells), bf16),
            pltpu.VMEM((2, 1, cells), f32),
            pltpu.VMEM((2, C, cells), bf16),
            pltpu.VMEM((1, cells), f32),
            pltpu.VMEM((2, C, cells), f32),
            pltpu.VMEM((2, C, cells), f32),
            pltpu.VMEM((2, C, cells), f32),
            pltpu.VMEM((2, C, cells), f32),
            pltpu.VMEM((2, C, cells), f32),
            pltpu.VMEM((C, cells), f32),
            pltpu.VMEM((2, C, cells), bf16),
            pltpu.VMEM((C, cells), f32),
            pltpu.VMEM((5 * C, cells), bf16),
            pltpu.VMEM((C, cells), f32),
            pltpu.SemaphoreType.DMA((EXCHANGES,)),
            pltpu.SemaphoreType.DMA((EXCHANGES,)),
            pltpu.SemaphoreType.DMA((EXCHANGES,)),
            pltpu.SemaphoreType.DMA((5,)),
        ],
        compiler_params=pltpu.CompilerParams(
            collective_id=0, has_side_effects=True, vmem_limit_bytes=60 * 2**20
        ),
    )(
        pair,
        grad_out,
        residue_chain,
        residue_chain.reshape(across, J),
        w_in,
        w_out,
        gain_in,
        gain_mid,
    )
    return pl.pallas_call(
        hand_on,
        out_shape=[jax.ShapeDtypeStruct(g.shape, g.dtype) for g in got],
        in_specs=[whole] * len(got),
        out_specs=[whole] * len(got),
    )(*got)


def solution(mesh):
    return jax.shard_map(
        partial(local, mesh.shape["chan"]),
        mesh=mesh,
        in_specs=(P("chan", "row", None), P("chan", "row", None), P(), P(), P(), P(), P()),
        out_specs=(P("chan", "row", None), P("chan", "row", None), P(), P(), P(), P()),
        check_vma=False,
    )
```
